32 devices in a mesh: lat: 4 (over y, x), col: 8 (over z, core).
Axes of the slice: x: 2, y: 2, z: 4, core: 2. Of those that a mesh axis runs over, the one named last changes fastest.
Arguments:
- control: float32 [128, 2048], P('lat', 'col'), may hold values from -6 to 6
- perturbations: float32 [128, 2048, 128], P('lat', 'col'), may hold values from -6 to 6
- zonal_flow: float32 [128, 2048], P('lat', 'col'), may hold values from -0.25 to 0.25
- meridional_flow: float32 [128, 2048], P('lat', 'col'), may hold values from -0.25 to 0.25
- diffusivity: float32 [128, 2048], P('lat', 'col'), may hold values from 0.03 to 0.12
- send_cell: int32 [4, 8, 8, 128], P('lat', 'col'), may hold values from 0 to 8191
- send_station: int32 [4, 8, 8, 128], P('lat', 'col'), may hold values from 0 to 255
- send_weight: float32 [4, 8, 8, 128], P('lat', 'col'), may hold values from 0.2 to 1
- send_count: int32 [4, 8, 8], P('lat', 'col'), may hold values from 32 to 128, as said below
- obs_value: float32 [2, 8192], P(None, ('lat', 'col')), may hold values from -24 to 24
- obs_error: float32 [2, 8192], P(None, ('lat', 'col')), may hold values from 1.3 to 64, as said below
Outputs:
- analysis: float32 [128, 2048, 128], P('lat', 'col')
- obs_analysis: float32 [2, 8192, 128], P(None, ('lat', 'col'))
The draws below stay inside these ranges and needn't reach their ends.
Inputs may be any that keep to these rules, and one draw needn't show every extreme that they name: send_count[l, e, d] counts the live leading slots that device e of latitude group l fills for device d of its group; in every group one device d receives all 128 slots from every source. obs_error is positive.
All inputs are finite; a program needn't handle non-finite values.
Results may differ from the reference program's by a relative error of at most 0.0003.
Values sent between devices are 32-bit elements; how exact they have to be, the bound alone decides.
A program may use at most 128 MiB of HBM per device.

```python
import math
import jax
import jax.numpy as jnp
from jax import lax

M = 128
CX = 32
CY = 256
OBS_DEV = 256
CAP = 128
STEPS = 2
NX = 128
NY = 2048
OBS = 8192
N_LAT = 4
N_COL = 8


def draw_send_count(key, part):
    key_base, key_busy = jax.random.split(key)
    counts = jax.random.randint(key_base, (N_LAT, N_COL, N_COL), CAP // 4, CAP + 1)
    busiest = jax.random.randint(key_busy, (N_LAT, 1, 1), 0, N_COL)
    column = jnp.arange(N_COL, dtype=jnp.int32)[None, None, :]
    return jnp.where(column == busiest, CAP, counts).astype(jnp.int32)


def draw_obs_error(key, part):
    placing = jnp.arange(OBS, dtype=jnp.float32) / OBS
    spread = jnp.exp(jax.random.uniform(key, (STEPS, OBS), jnp.float32, jnp.log(4.0), jnp.log(64.0)))
    return (spread * jnp.exp(-jnp.log(3.0) * placing)[None, :]).astype(jnp.float32)


def with_ends(entries, key, smallest, largest):
    place = [jax.random.randint(jax.random.fold_in(key, axis), (), 0, length) for axis, length in enumerate(entries.shape)]
    main_axis = entries.shape.index(max(entries.shape))
    beside = place[:main_axis] + [(place[main_axis] + 1) % entries.shape[main_axis]] + place[main_axis + 1:]
    return entries.at[tuple(place)].set(smallest).at[tuple(beside)].set(largest)


def block_levels(stream_key, dims, pieces, low, largest):
    loudness, own = 1.0, jax.random.fold_in(stream_key, 6)
    for position, parts in pieces:
        heights = jnp.exp(jax.random.uniform(jax.random.fold_in(own, position), (parts,), jnp.float32, low / len(pieces), largest / len(pieces)))
        loudness = loudness * jnp.repeat(heights, dims[position] // parts).reshape([-1 if axis == position else 1 for axis in range(len(dims))])
    return loudness


def bell_draw(key, dims, scale, limit, cuts=(), kind=jnp.bfloat16):
    values = scale * jax.random.normal(key, dims, jnp.float32)
    if cuts:
        values = values * block_levels(key, dims, cuts, -0.22, 0.18)
    return jnp.clip(values, -limit, limit).astype(kind)


def setup_inputs(seed: int = 0) -> dict:
    streams_of = jax.random.split(jax.random.key(seed), 12)
    return {
        "control": bell_draw(streams_of[0], (NX, NY), 1.0, 6.0, ((0, 4), (1, 8)), jnp.float32),
        "perturbations": bell_draw(streams_of[1], (NX, NY, M), 1.0, 6.0, ((0, 4), (1, 8)), jnp.float32),
        "zonal_flow": jnp.clip(jax.random.uniform(streams_of[2], (NX, NY), jnp.float32, -0.25, 0.25) * block_levels(streams_of[2], (NX, NY), ((0, 4), (1, 8)), -0.4, 0.0), -0.25, 0.25),
        "meridional_flow": jnp.clip(jax.random.uniform(streams_of[3], (NX, NY), jnp.float32, -0.25, 0.25) * block_levels(streams_of[3], (NX, NY), ((0, 4), (1, 8)), -0.4, 0.0), -0.25, 0.25),
        "diffusivity": jnp.clip(jnp.exp(math.log(0.12) - 1.3862944 * jax.random.uniform(streams_of[4], (NX, NY), jnp.float32) ** block_levels(streams_of[4], (NX, NY), ((0, 4), (1, 8)), -0.2, 0.2)), 0.03, 0.12),
        "send_cell": with_ends(jax.random.randint(streams_of[5], (N_LAT, N_COL, N_COL, CAP), 0, CX * CY), jax.random.fold_in(streams_of[5], 1), 0, (CX * CY) - 1).astype(jnp.int32),
        "send_station": with_ends(jax.random.randint(streams_of[6], (N_LAT, N_COL, N_COL, CAP), 0, OBS_DEV), jax.random.fold_in(streams_of[6], 1), 0, OBS_DEV - 1).astype(jnp.int32),
        "send_weight": jnp.clip(0.2 + 0.8 * jax.random.uniform(streams_of[7], (N_LAT, N_COL, N_COL, CAP), jnp.float32) ** block_levels(streams_of[7], (N_LAT, N_COL, N_COL, CAP), ((0, 4), (1, 8)), -0.2, 0.2), 0.2, 1.0),
        "send_count": draw_send_count(jax.random.fold_in(streams_of[11], 71), 0),
        "obs_value": bell_draw(streams_of[9], (STEPS, OBS), 4.0, 24.0, ((1, 32),), jnp.float32),
        "obs_error": draw_obs_error(jax.random.fold_in(streams_of[11], 71), 0),
    }


exact_mode = lax.Precision.HIGHEST

def upwind_rates(zonal, meridional, diffusion):
    east_rate = diffusion + jnp.maximum(-zonal, 0.0)
    west_rate = diffusion + jnp.maximum(zonal, 0.0)
    north_rate = diffusion + jnp.maximum(-meridional, 0.0)
    south_rate = diffusion + jnp.maximum(meridional, 0.0)
    return (east_rate[..., None], west_rate[..., None], north_rate[..., None], south_rate[..., None])

def advance(padded, coeffs):
    centre = padded[1:-1, 1:-1]
    result = centre + coeffs[0] * (padded[2:, 1:-1] - centre)
    result = result + coeffs[1] * (padded[:-2, 1:-1] - centre)
    result = result + coeffs[2] * (padded[1:-1, 2:] - centre)
    return result + coeffs[3] * (padded[1:-1, :-2] - centre)

def reference(control, perturbations, zonal_flow, meridional_flow, diffusivity, send_cell, send_station, send_weight, send_count, obs_value, obs_error):
    members = perturbations + control[:, :, None]
    coeffs = upwind_rates(zonal_flow, meridional_flow, diffusivity)
    prior_ensemble_matrix = []
    current_model_vector = members
    for time_index in range(STEPS):
        padded = jnp.pad(current_model_vector, ((1, 1), (1, 1), (0, 0)))
        current_model_vector = advance(padded, coeffs)
        prior_ensemble_matrix.append(current_model_vector)
    live_slot = jnp.arange(CAP, dtype=jnp.int32)[None, None, None, :] < send_count[..., None]
    factors = jnp.where(live_slot, send_weight, 0.0)
    destination = jnp.arange(N_COL, dtype=jnp.int32)[:, None]
    zero_index = jnp.zeros((), jnp.int32)

    def measure_operator(field):

        def visit(totals, source_id):
            lat_group = source_id // N_COL
            sender = source_id % N_COL
            device_block = lax.dynamic_slice(field, (lat_group * CX, sender * CY, zero_index), (CX, CY, M)).reshape(CX * CY, M)
            cell_ids = send_cell[lat_group, sender].reshape(-1)
            picked = device_block[cell_ids] * factors[lat_group, sender].reshape(-1)[:, None]
            target = ((lat_group * N_COL + destination) * OBS_DEV + send_station[lat_group, sender]).reshape(-1)
            return (totals.at[target].add(picked), None)
        result, unused = lax.scan(visit, jnp.zeros((OBS, M), jnp.float32), jnp.arange(N_LAT * N_COL, dtype=jnp.int32))
        return result
    root_scale = math.sqrt(M - 1.0)
    gram = jnp.eye(M, dtype=jnp.float32)
    push = jnp.zeros((M,), jnp.float32)
    means = []
    spreads = []
    for time_index in range(STEPS):
        measurement_vector = measure_operator(prior_ensemble_matrix[time_index])
        obs_mean = lax.optimization_barrier(jnp.mean(measurement_vector, axis=1))
        spread = measurement_vector - obs_mean[:, None]
        scaled = spread / (obs_error[time_index][:, None] * root_scale)
        innovation = (obs_value[time_index] - obs_mean) / obs_error[time_index]
        gram = gram + jnp.dot(scaled.T, scaled, precision=exact_mode)
        push = push + jnp.dot(innovation, scaled, precision=exact_mode)
        means.append(obs_mean)
        spreads.append(spread)
    factor = jnp.linalg.cholesky(gram)
    identity = jnp.eye(M, dtype=jnp.float32)
    inverse = lax.linalg.triangular_solve(factor, identity, left_side=True, lower=True)
    offset = jnp.dot(inverse.T, jnp.dot(inverse, push, precision=exact_mode), precision=exact_mode) / root_scale
    weights = inverse.T + offset[:, None]
    final_model_vector = prior_ensemble_matrix[-1]
    state_mean = lax.optimization_barrier(jnp.mean(final_model_vector, axis=2, keepdims=True))
    departures = (final_model_vector - state_mean).reshape(-1, M)
    analysis = state_mean + jnp.dot(departures, weights, precision=exact_mode).reshape(final_model_vector.shape)
    obs_analysis = jnp.stack([means[k][:, None] + jnp.dot(spreads[k], weights, precision=exact_mode) for k in range(STEPS)])
    return (analysis, obs_analysis)
```

```python
import functools
import math

import jax
import jax.numpy as jnp
from jax import lax
from jax.experimental import pallas as pl
from jax.experimental.pallas import tpu as pltpu
from jax.sharding import PartitionSpec as P

MESH = pl.DeviceIdType.MESH
exact_mode = lax.Precision.HIGHEST
PAD = 8


def slice_rows(members, count):
    return -(-(members + 1) // (8 * count)) * 8


def forecast_kernel(
    n_lat,
    n_col,
    control,
    perturbations,
    zonal,
    meridional,
    diffusion,
    cell,
    station,
    weight,
    live,
    obs_value,
    obs_error,
    final_out,
    observed_out,
    total_out,
    state_0,
    state_1,
    state_2,
    rates,
    columns,
    edge_send,
    edge_recv,
    side_recv,
    slots_send,
    slots_recv,
    part,
    part_recv,
    lat_part,
    total,
    load_sem,
    store_sem,
    halo_send_sem,
    halo_recv_sem,
    slots_send_sem,
    slots_recv_sem,
    part_send_sem,
    part_recv_sem,
    lat_send_sem,
    lat_recv_sem,
    total_send_sem,
    total_recv_sem,
):
    lat, col = lax.axis_index("lat"), lax.axis_index("col")
    nx, ny = control.shape
    m = perturbations.shape[2]
    cap = cell.shape[1]
    steps, owned = obs_value.shape
    states = (state_0, state_1, state_2)

    chunk = nx // 4
    loads = [
        pltpu.make_async_copy(
            perturbations.at[pl.ds(q * chunk, chunk)],
            state_0.at[pl.ds(1 + q * chunk, chunk), pl.ds(PAD, ny)],
            load_sem.at[q],
        )
        for q in range(4)
    ]
    for q in (0, 3, 1, 2):
        loads[q].start()

    barrier = pltpu.get_barrier_semaphore()

    def greet_col(o, carry):
        pl.semaphore_signal(barrier, inc=1, device_id=(lat, lax.rem(col + o, n_col)), device_id_type=MESH)
        return carry

    def greet_lat(o, carry):
        pl.semaphore_signal(barrier, inc=1, device_id=(lax.rem(lat + o, n_lat), col), device_id_type=MESH)
        return carry

    lax.fori_loop(1, n_col, greet_col, 0)
    lax.fori_loop(1, n_lat, greet_lat, 0)

    u, v, d = zonal[...], meridional[...], diffusion[...]
    fields = [
        d + jnp.maximum(-u, 0.0),
        d + jnp.maximum(u, 0.0),
        d + jnp.maximum(-v, 0.0),
        d + jnp.maximum(v, 0.0),
    ]
    rates[...] = jnp.transpose(jnp.concatenate(fields, axis=0))
    rest = jnp.zeros((128 - nx - 2 * steps, ny), jnp.float32)
    columns[...] = jnp.transpose(jnp.concatenate([control[...], obs_value[...], obs_error[...], rest], axis=0))

    def edges(t, i, low, high):
        edge_send[t, 0, pl.ds(i, 1), :] = low
        edge_send[t, 1, pl.ds(i, 1), :] = high

    def add_row(i, carry):
        shift = lax.rem(128 - i, 128)
        for j in range(0, ny, 64):
            centre = pltpu.roll(columns[j : j + 64, :], shift, 1)[:, 0:1]
            value = state_0[1 + i, PAD + j : PAD + j + 64, :] + centre
            state_0[1 + i, PAD + j : PAD + j + 64, :] = value
            if j == 0:
                edge_send[0, 0, pl.ds(i, 1), :] = value[0:1]
            if j == ny - 64:
                edge_send[0, 1, pl.ds(i, 1), :] = value[63:64]
        return carry

    def halo(t, side):
        source = states[t]
        if side == 0:
            src, dst, to = source.at[1, pl.ds(PAD, ny)], side_recv.at[t, 1], (lat - 1, col)
        elif side == 1:
            src, dst, to = source.at[nx, pl.ds(PAD, ny)], side_recv.at[t, 0], (lat + 1, col)
        elif side == 2:
            src, dst, to = edge_send.at[t, 0], edge_recv.at[t, 1], (lat, col - 1)
        else:
            src, dst, to = edge_send.at[t, 1], edge_recv.at[t, 0], (lat, col + 1)
        arrives = side ^ 1
        send = pltpu.make_async_remote_copy(
            src_ref=src,
            dst_ref=dst,
            send_sem=halo_send_sem.at[t, side],
            recv_sem=halo_recv_sem.at[t, arrives],
            device_id=to,
            device_id_type=MESH,
        )
        return send

    exists = (lat > 0, lat < n_lat - 1, col > 0, col < n_col - 1)

    def send_halo(t, side):
        @pl.when(exists[side])
        def _():
            halo(t, side).start()

    def take_halo(t, side):
        target = states[t]

        @pl.when(exists[side])
        def _():
            halo(t, side ^ 1).wait_recv()
            if side < 2:
                target[(nx + 1) * side, PAD : PAD + ny, :] = side_recv[t, side]
            else:
                at = PAD - 1 if side == 2 else PAD + ny

                def put(i, carry):
                    target[1 + i, at : at + 1, :] = edge_recv[t, side - 2, pl.ds(i, 1), :]
                    return carry

                lax.fori_loop(0, nx, put, 0)

        @pl.when(jnp.logical_not(exists[side]))
        def _():
            if side < 2:
                target[(nx + 1) * side, PAD : PAD + ny, :] = jnp.zeros((ny, m), jnp.float32)
            else:
                at = PAD - 1 if side == 2 else PAD + ny

                def put(i, carry):
                    target[1 + i, at : at + 1, :] = jnp.zeros((1, m), jnp.float32)
                    return carry

                lax.fori_loop(0, nx, put, 0)

    def step_row(t, i, carry):
        source, target = states[t], states[t + 1]
        shift = lax.rem(128 - i, 128)
        for j in range(0, ny, 64):
            k = pltpu.roll(rates[j : j + 64, :], shift, 1)
            at = PAD + j
            centre = source[1 + i, at : at + 64, :]
            value = centre + k[:, 0:1] * (source[2 + i, at : at + 64, :] - centre)
            value = value + k[:, nx : nx + 1] * (source[i, at : at + 64, :] - centre)
            value = value + k[:, 2 * nx : 2 * nx + 1] * (source[1 + i, at + 1 : at + 65, :] - centre)
            value = value + k[:, 3 * nx : 3 * nx + 1] * (source[1 + i, at - 1 : at + 63, :] - centre)
            target[1 + i, at : at + 64, :] = value
            if t + 1 < steps:
                if j == 0:
                    edge_send[t + 1, 0, pl.ds(i, 1), :] = value[0:1]
                if j == ny - 64:
                    edge_send[t + 1, 1, pl.ds(i, 1), :] = value[63:64]
        return carry

    def slot_copy(t, o):
        rows = cap + 8 if t == 0 else cap
        return pltpu.make_async_remote_copy(
            src_ref=slots_send.at[t, o, pl.ds(0, rows)],
            dst_ref=slots_recv.at[t, o, pl.ds(0, rows)],
            send_sem=slots_send_sem.at[t, o],
            recv_sem=slots_recv_sem.at[t, o],
            device_id=(lat, lax.rem(col + o, n_col)),
            device_id_type=MESH,
        )

    bits = ny.bit_length() - 1

    def fill(t, o):
        source = states[t + 1]
        receiver = lax.rem(col + o, n_col)

        def group(g, carry):
            for r in range(16):
                c = cell[receiver, g * 16 + r]
                i, j = lax.shift_right_logical(c, bits), c & (ny - 1)
                slots_send[t, o, pl.ds(g * 16 + r, 1), :] = source[1 + i, pl.ds(PAD + j, 1), :]
            return carry

        lax.fori_loop(0, cap // 16, group, 0)
        if t == 0:
            lane = lax.broadcasted_iota(jnp.int32, (1, cap), 1)
            factor = jnp.where(lane < live[0, receiver], weight[pl.ds(receiver, 1), :], 0.0)
            line = lax.broadcasted_iota(jnp.int32, (8, cap), 0)
            head = jnp.where(line == 0, station[pl.ds(receiver, 1), :].astype(jnp.float32), factor)
            slots_send[t, o, pl.ds(cap, 8), :] = head

    def nth(k):
        half = lax.div(k + 1, 2)
        return n_col // 2 + jnp.where(lax.rem(k, 2) == 1, -half, half)

    def send_slots(t):
        def one(k, carry):
            o = nth(k)
            fill(t, o)
            slot_copy(t, o).start()
            return carry

        lax.fori_loop(0, n_col - 1, one, 0)
        fill(t, 0)

    loads[0].wait()
    loads[3].wait()
    add_row(0, 0)
    add_row(nx - 1, 0)
    pl.semaphore_wait(barrier, n_col + n_lat - 2)
    send_halo(0, 0)
    send_halo(0, 1)
    loads[1].wait()
    loads[2].wait()
    lax.fori_loop(1, nx - 1, add_row, 0)
    send_halo(0, 2)
    send_halo(0, 3)

    for t in range(steps):
        take_halo(t, 2)
        take_halo(t, 3)
        lax.fori_loop(1, nx - 1, functools.partial(step_row, t), 0)
        take_halo(t, 0)
        take_halo(t, 1)
        step_row(t, 0, 0)
        step_row(t, nx - 1, 0)
        if t + 1 < steps:
            for side in range(4):
                send_halo(t + 1, side)
        send_slots(t)
    store = pltpu.make_async_copy(state_2.at[pl.ds(1, nx), pl.ds(PAD, ny)], final_out, store_sem)
    store.start()

    root_scale = math.sqrt(m - 1.0)
    part[...] = jnp.zeros_like(part)
    gram = jnp.zeros((m, m), jnp.float32)
    push = jnp.zeros((1, m), jnp.float32)
    for t in range(steps):
        line = lax.broadcasted_iota(jnp.int32, (owned, cap), 0).astype(jnp.float32)

        def product(head, values):
            mix = jnp.where(line == head[0:1], head[1:2], 0.0)
            return jnp.dot(mix, values, precision=exact_mode, preferred_element_type=jnp.float32)

        observed_out[t] = product(slots_send[0, 0, pl.ds(cap, 8), :], slots_send[t, 0, pl.ds(0, cap), :])

        def one(k, carry):
            o = nth(n_col - 2 - k)
            slot_copy(t, o).wait_recv()
            observed_out[t] += product(slots_recv[0, o, pl.ds(cap, 8), :], slots_recv[t, o, pl.ds(0, cap), :])
            return carry

        lax.fori_loop(0, n_col - 1, one, 0)
        observed = observed_out[t]
        mean = jnp.mean(observed, axis=1, keepdims=True)
        spread = observed - mean
        error = columns[:, nx + steps + t : nx + steps + t + 1]
        scaled = spread / (error * root_scale)
        innovation = (columns[:, nx + t : nx + t + 1] - mean) / error
        gram = gram + lax.dot_general(
            scaled, scaled, (((0,), (0,)), ((), ())), precision=exact_mode, preferred_element_type=jnp.float32
        )
        push = push + jnp.sum(scaled * innovation, axis=0, keepdims=True)
    part[0:m, :] = gram
    part[m : m + 1, :] = push

    rows = part_recv.shape[1]

    def mine(ref, who):
        return ref.at[pl.ds(pl.multiple_of(who * rows, 8), rows)]

    def part_copy(o):
        who = lax.rem(col + o, n_col)
        return pltpu.make_async_remote_copy(
            src_ref=mine(part, who),
            dst_ref=part_recv.at[o],
            send_sem=part_send_sem.at[o],
            recv_sem=part_recv_sem.at[o],
            device_id=(lat, who),
            device_id_type=MESH,
        )

    def lat_copy(o):
        return pltpu.make_async_remote_copy(
            src_ref=lat_part.at[0],
            dst_ref=lat_part.at[o],
            send_sem=lat_send_sem.at[o],
            recv_sem=lat_recv_sem.at[o],
            device_id=(lax.rem(lat + o, n_lat), col),
            device_id_type=MESH,
        )

    def total_copy(o, owner):
        return pltpu.make_async_remote_copy(
            src_ref=mine(total, owner),
            dst_ref=mine(total, owner),
            send_sem=total_send_sem.at[o],
            recv_sem=total_recv_sem.at[o],
            device_id=(lat, lax.rem(col + o, n_col)),
            device_id_type=MESH,
        )

    def each(count, act):
        def body(o, carry):
            act(o)
            return carry

        lax.fori_loop(1, count, body, 0)

    each(n_col, lambda o: part_copy(o).start())
    here = pl.ds(pl.multiple_of(col * rows, 8), rows)

    def add_part(o, acc):
        part_copy(o).wait_recv()
        return acc + part_recv[o]

    lat_part[0] = lax.fori_loop(1, n_col, add_part, part[here, :])
    each(n_lat, lambda o: lat_copy(o).start())

    def add_lat(o, acc):
        lat_copy(o).wait_recv()
        return acc + lat_part[o]

    total[here, :] = lax.fori_loop(1, n_lat, add_lat, lat_part[0])
    each(n_col, lambda o: total_copy(o, col).start())
    each(n_col, lambda o: total_copy(o, lax.rem(col + n_col - o, n_col)).wait_recv())
    total_out[...] = total[...]

    each(n_col, lambda o: part_copy(o).wait_send())
    each(n_lat, lambda o: lat_copy(o).wait_send())
    each(n_col, lambda o: total_copy(o, col).wait_send())
    for t in range(steps):
        each(n_col, lambda o: slot_copy(t, o).wait_send())
        for side in range(4):

            @pl.when(exists[side])
            def _():
                halo(t, side).wait_send()

    store.wait()


def on_device(
    n_lat,
    n_col,
    control,
    perturbations,
    zonal_flow,
    meridional_flow,
    diffusivity,
    send_cell,
    send_station,
    send_weight,
    send_count,
    obs_value,
    obs_error,
):
    nx, ny, m = perturbations.shape
    cap = send_cell.shape[3]
    steps, owned = obs_value.shape
    rows = slice_rows(m, n_col)
    f32 = jnp.float32
    state = pltpu.VMEM((nx + 2, ny + 2 * PAD, m), f32)
    dma = pltpu.SemaphoreType.DMA
    vmem, smem, anywhere = (pl.BlockSpec(memory_space=s) for s in (pltpu.VMEM, pltpu.SMEM, pl.ANY))
    final, observed, total = pl.pallas_call(
        functools.partial(forecast_kernel, n_lat, n_col),
        out_shape=(
            jax.ShapeDtypeStruct((nx, ny, m), f32),
            jax.ShapeDtypeStruct((steps, owned, m), f32),
            jax.ShapeDtypeStruct((n_col * rows, m), f32),
        ),
        in_specs=[vmem, anywhere, vmem, vmem, vmem, smem, vmem, vmem, smem, vmem, vmem],
        out_specs=(anywhere, vmem, vmem),
        scratch_shapes=[
            state,
            state,
            state,
            pltpu.VMEM((ny, 128), f32),
            pltpu.VMEM((ny, 128), f32),
            pltpu.VMEM((steps, 2, nx, m), f32),
            pltpu.VMEM((steps, 2, nx, m), f32),
            pltpu.VMEM((steps, 2, ny, m), f32),
            pltpu.VMEM((steps, n_col, cap + 8, m), f32),
            pltpu.VMEM((steps, n_col, cap + 8, m), f32),
            pltpu.VMEM((n_col * rows, m), f32),
            pltpu.VMEM((n_col, rows, m), f32),
            pltpu.VMEM((n_lat, rows, m), f32),
            pltpu.VMEM((n_col * rows, m), f32),
            dma((4,)),
            dma,
            dma((steps, 4)),
            dma((steps, 4)),
            dma((steps, n_col)),
            dma((steps, n_col)),
            dma((n_col,)),
            dma((n_col,)),
            dma((n_lat,)),
            dma((n_lat,)),
            dma((n_col,)),
            dma((n_col,)),
        ],
        compiler_params=pltpu.CompilerParams(
            collective_id=0, has_side_effects=True, vmem_limit_bytes=48 * 1024 * 1024
        ),
    )(
        control,
        perturbations,
        zonal_flow,
        meridional_flow,
        diffusivity,
        send_cell[0, 0],
        send_station[0, 0],
        send_weight[0, 0],
        send_count[0],
        obs_value,
        obs_error,
    )
    root_scale = math.sqrt(m - 1.0)
    identity = jnp.eye(m, dtype=f32)
    push = total[m]
    factor = jnp.linalg.cholesky(identity + total[:m])
    inverse = lax.linalg.triangular_solve(factor, identity, left_side=True, lower=True)
    offset = (
        jnp.dot(inverse.T, jnp.dot(inverse, push, precision=exact_mode), precision=exact_mode) / root_scale
    )
    weights = inverse.T + offset[:, None]

    def transform(values):
        mean = jnp.mean(values, axis=-1, keepdims=True)
        return mean + jnp.dot(
            (values - mean).reshape(-1, m), weights, precision=exact_mode
        ).reshape(values.shape)

    return transform(final), transform(observed)


def solution(mesh):
    n_lat, n_col = mesh.shape["lat"], mesh.shape["col"]
    return jax.shard_map(
        functools.partial(on_device, n_lat, n_col),
        mesh=mesh,
        in_specs=(
            P("lat", "col"),
            P("lat", "col", None),
            P("lat", "col"),
            P("lat", "col"),
            P("lat", "col"),
            P("lat", "col", None, None),
            P("lat", "col", None, None),
            P("lat", "col", None, None),
            P("lat", "col", None),
            P(None, ("lat", "col")),
            P(None, ("lat", "col")),
        ),
        out_specs=(P("lat", "col", None), P(None, ("lat", "col"), None)),
        check_vma=False,
    )
```

```python
import functools
import math

import jax
import jax.numpy as jnp
from jax import lax
from jax.experimental import pallas as pl
from jax.experimental.pallas import tpu as pltpu
from jax.sharding import PartitionSpec as P

MESH = pl.DeviceIdType.MESH
exact_mode = lax.Precision.HIGHEST
PAD = 8


def slice_rows(members, count):
    return -(-(members + 1) // (8 * count)) * 8


def forecast_kernel(
    n_lat,
    n_col,
    control_in,
    perturbations,
    zonal_in,
    meridional_in,
    diffusion_in,
    cell_in,
    station_in,
    weight_in,
    live_in,
    obs_value_in,
    obs_error_in,
    final_out,
    observed_store,
    total_out,
    control,
    zonal,
    meridional,
    diffusion,
    cell,
    station,
    weight,
    live,
    obs_value,
    obs_error,
    observed_out,
    wide,
    state_0,
    state_1,
    state_2,
    rates,
    columns,
    edge_send,
    edge_recv,
    side_recv,
    slots_send,
    slots_recv,
    part,
    part_recv,
    lat_part,
    total,
    small_sem,
    load_sem,
    store_sem,
    halo_send_sem,
    halo_recv_sem,
    slots_send_sem,
    slots_recv_sem,
    part_send_sem,
    part_recv_sem,
    lat_send_sem,
    lat_recv_sem,
    total_send_sem,
    total_recv_sem,
):
    lat, col = lax.axis_index("lat"), lax.axis_index("col")
    nx, ny = control.shape
    m = perturbations.shape[2]
    cap = cell.shape[1]
    steps, owned = obs_value.shape
    states = (state_0, state_1, state_2)

    chunk = nx // 4
    loads = [
        pltpu.make_async_copy(
            perturbations.at[pl.ds(q * chunk, chunk)],
            state_0.at[pl.ds(1 + q * chunk, chunk), pl.ds(PAD, ny)],
            load_sem.at[q],
        )
        for q in range(4)
    ]
    pairs = (
        (zonal_in, zonal),
        (meridional_in, meridional),
        (diffusion_in, diffusion),
        (control_in, control),
        (obs_value_in, obs_value),
        (obs_error_in, obs_error),
        (cell_in, cell),
        (live_in, live),
        (station_in, station),
        (weight_in, weight),
    )
    smalls = [pltpu.make_async_copy(a, b, small_sem.at[q]) for q, (a, b) in enumerate(pairs)]
    for copy in smalls:
        copy.start()
    for q in (0, 3, 1, 2):
        loads[q].start()

    barrier = pltpu.get_barrier_semaphore()

    def greet_col(o, carry):
        pl.semaphore_signal(barrier, inc=1, device_id=(lat, lax.rem(col + o, n_col)), device_id_type=MESH)
        return carry

    def greet_lat(o, carry):
        pl.semaphore_signal(barrier, inc=1, device_id=(lax.rem(lat + o, n_lat), col), device_id_type=MESH)
        return carry

    lax.fori_loop(1, n_col, greet_col, 0)
    lax.fori_loop(1, n_lat, greet_lat, 0)

    for copy in smalls:
        copy.wait()
    u, v, d = zonal[...], meridional[...], diffusion[...]
    fields = [
        d + jnp.maximum(-u, 0.0),
        d + jnp.maximum(u, 0.0),
        d + jnp.maximum(-v, 0.0),
        d + jnp.maximum(v, 0.0),
    ]
    rates[...] = jnp.transpose(jnp.concatenate(fields, axis=0))
    rest = jnp.zeros((128 - nx - 2 * steps, ny), jnp.float32)
    columns[...] = jnp.transpose(jnp.concatenate([control[...], obs_value[...], obs_error[...], rest], axis=0))

    def widen(i, carry):
        shift = lax.rem(128 - i, 128)
        for j in range(0, ny, 64):
            k = pltpu.roll(rates[j : j + 64, :], shift, 1)
            for q in range(4):
                wide[q, i, j : j + 64, :] = jnp.broadcast_to(k[:, q * nx : q * nx + 1], (64, m))
        return carry

    def add_row(i, carry):
        shift = lax.rem(128 - i, 128)
        for j in range(0, ny, 64):
            centre = pltpu.roll(columns[j : j + 64, :], shift, 1)[:, 0:1]
            value = state_0[1 + i, PAD + j : PAD + j + 64, :] + centre
            state_0[1 + i, PAD + j : PAD + j + 64, :] = value
            if j == 0:
                edge_send[0, 0, pl.ds(i, 1), :] = value[0:1]
            if j == ny - 64:
                edge_send[0, 1, pl.ds(i, 1), :] = value[63:64]
        return carry

    def halo(t, side):
        source = states[t]
        if side == 0:
            src, dst, to = source.at[1, pl.ds(PAD, ny)], side_recv.at[t, 1], (lat - 1, col)
        elif side == 1:
            src, dst, to = source.at[nx, pl.ds(PAD, ny)], side_recv.at[t, 0], (lat + 1, col)
        elif side == 2:
            src, dst, to = edge_send.at[t, 0], edge_recv.at[t, 1], (lat, col - 1)
        else:
            src, dst, to = edge_send.at[t, 1], edge_recv.at[t, 0], (lat, col + 1)
        arrives = side ^ 1
        send = pltpu.make_async_remote_copy(
            src_ref=src,
            dst_ref=dst,
            send_sem=halo_send_sem.at[t, side],
            recv_sem=halo_recv_sem.at[t, arrives],
            device_id=to,
            device_id_type=MESH,
        )
        return send

    exists = (lat > 0, lat < n_lat - 1, col > 0, col < n_col - 1)

    def send_halo(t, side):
        @pl.when(exists[side])
        def _():
            halo(t, side).start()

    def take_halo(t, side):
        target = states[t]

        @pl.when(exists[side])
        def _():
            halo(t, side ^ 1).wait_recv()
            if side < 2:
                target[(nx + 1) * side, PAD : PAD + ny, :] = side_recv[t, side]
            else:
                at = PAD - 1 if side == 2 else PAD + ny

                def put(i, carry):
                    target[1 + i, at : at + 1, :] = edge_recv[t, side - 2, pl.ds(i, 1), :]
                    return carry

                lax.fori_loop(0, nx, put, 0)

        @pl.when(jnp.logical_not(exists[side]))
        def _():
            if side < 2:
                target[(nx + 1) * side, PAD : PAD + ny, :] = jnp.zeros((ny, m), jnp.float32)
            else:
                at = PAD - 1 if side == 2 else PAD + ny

                def put(i, carry):
                    target[1 + i, at : at + 1, :] = jnp.zeros((1, m), jnp.float32)
                    return carry

                lax.fori_loop(0, nx, put, 0)

    def step_row(t, i, carry):
        source, target = states[t], states[t + 1]
        for j in range(0, ny, 64):
            k = [wide[q, i, j : j + 64, :] for q in range(4)]
            at = PAD + j
            centre = source[1 + i, at : at + 64, :]
            value = centre + k[0] * (source[2 + i, at : at + 64, :] - centre)
            value = value + k[1] * (source[i, at : at + 64, :] - centre)
            value = value + k[2] * (source[1 + i, at + 1 : at + 65, :] - centre)
            value = value + k[3] * (source[1 + i, at - 1 : at + 63, :] - centre)
            target[1 + i, at : at + 64, :] = value
            if t + 1 < steps:
                if j == 0:
                    edge_send[t + 1, 0, pl.ds(i, 1), :] = value[0:1]
                if j == ny - 64:
                    edge_send[t + 1, 1, pl.ds(i, 1), :] = value[63:64]
        return carry

    def slot_copy(t, o):
        rows = cap + 8 if t == 0 else cap
        return pltpu.make_async_remote_copy(
            src_ref=slots_send.at[t, o, pl.ds(0, rows)],
            dst_ref=slots_recv.at[t, o, pl.ds(0, rows)],
            send_sem=slots_send_sem.at[t, o],
            recv_sem=slots_recv_sem.at[t, o],
            device_id=(lat, lax.rem(col + o, n_col)),
            device_id_type=MESH,
        )

    bits = ny.bit_length() - 1

    def fill(t, o):
        source = states[t + 1]
        receiver = lax.rem(col + o, n_col)

        def group(g, carry):
            for r in range(16):
                c = cell[receiver, g * 16 + r]
                i, j = lax.shift_right_logical(c, bits), c & (ny - 1)
                slots_send[t, o, pl.ds(g * 16 + r, 1), :] = source[1 + i, pl.ds(PAD + j, 1), :]
            return carry

        lax.fori_loop(0, cap // 16, group, 0)
        if t == 0:
            lane = lax.broadcasted_iota(jnp.int32, (1, cap), 1)
            factor = jnp.where(lane < live[0, receiver], weight[pl.ds(receiver, 1), :], 0.0)
            line = lax.broadcasted_iota(jnp.int32, (8, cap), 0)
            head = jnp.where(line == 0, station[pl.ds(receiver, 1), :].astype(jnp.float32), factor)
            slots_send[t, o, pl.ds(cap, 8), :] = head

    def nth(k):
        half = lax.div(k + 1, 2)
        return n_col // 2 + jnp.where(lax.rem(k, 2) == 1, -half, half)

    def send_slots(t):
        def one(k, carry):
            o = nth(k)
            fill(t, o)
            slot_copy(t, o).start()
            return carry

        lax.fori_loop(0, n_col - 1, one, 0)
        fill(t, 0)

    loads[0].wait()
    loads[3].wait()
    add_row(0, 0)
    add_row(nx - 1, 0)
    pl.semaphore_wait(barrier, n_col + n_lat - 2)
    send_halo(0, 0)
    send_halo(0, 1)
    loads[1].wait()
    loads[2].wait()
    lax.fori_loop(1, nx - 1, add_row, 0)
    send_halo(0, 2)
    send_halo(0, 3)
    lax.fori_loop(0, nx, widen, 0)

    for t in range(steps):
        take_halo(t, 2)
        take_halo(t, 3)
        lax.fori_loop(1, nx - 1, functools.partial(step_row, t), 0)
        take_halo(t, 0)
        take_halo(t, 1)
        step_row(t, 0, 0)
        step_row(t, nx - 1, 0)
        if t + 1 < steps:
            for side in range(4):
                send_halo(t + 1, side)
        send_slots(t)
    store = pltpu.make_async_copy(state_2.at[pl.ds(1, nx), pl.ds(PAD, ny)], final_out, store_sem.at[0])
    store.start()

    root_scale = math.sqrt(m - 1.0)
    part[...] = jnp.zeros_like(part)
    gram = jnp.zeros((m, m), jnp.float32)
    push = jnp.zeros((1, m), jnp.float32)
    for t in range(steps):
        line = lax.broadcasted_iota(jnp.int32, (owned, cap), 0).astype(jnp.float32)

        def product(head, values):
            mix = jnp.where(line == head[0:1], head[1:2], 0.0)
            return jnp.dot(mix, values, precision=exact_mode, preferred_element_type=jnp.float32)

        observed_out[t] = product(slots_send[0, 0, pl.ds(cap, 8), :], slots_send[t, 0, pl.ds(0, cap), :])

        def one(k, carry):
            o = nth(n_col - 2 - k)
            slot_copy(t, o).wait_recv()
            observed_out[t] += product(slots_recv[0, o, pl.ds(cap, 8), :], slots_recv[t, o, pl.ds(0, cap), :])
            return carry

        lax.fori_loop(0, n_col - 1, one, 0)
        observed = observed_out[t]
        mean = jnp.mean(observed, axis=1, keepdims=True)
        spread = observed - mean
        error = columns[:, nx + steps + t : nx + steps + t + 1]
        scaled = spread / (error * root_scale)
        innovation = (columns[:, nx + t : nx + t + 1] - mean) / error
        gram = gram + lax.dot_general(
            scaled, scaled, (((0,), (0,)), ((), ())), precision=exact_mode, preferred_element_type=jnp.float32
        )
        push = push + jnp.sum(scaled * innovation, axis=0, keepdims=True)
    part[0:m, :] = gram
    part[m : m + 1, :] = push

    rows = part_recv.shape[1]

    def mine(ref, who):
        return ref.at[pl.ds(pl.multiple_of(who * rows, 8), rows)]

    def part_copy(o):
        who = lax.rem(col + o, n_col)
        return pltpu.make_async_remote_copy(
            src_ref=mine(part, who),
            dst_ref=part_recv.at[o],
            send_sem=part_send_sem.at[o],
            recv_sem=part_recv_sem.at[o],
            device_id=(lat, who),
            device_id_type=MESH,
        )

    def lat_copy(o):
        return pltpu.make_async_remote_copy(
            src_ref=lat_part.at[0],
            dst_ref=lat_part.at[o],
            send_sem=lat_send_sem.at[o],
            recv_sem=lat_recv_sem.at[o],
            device_id=(lax.rem(lat + o, n_lat), col),
            device_id_type=MESH,
        )

    def total_copy(o, owner):
        return pltpu.make_async_remote_copy(
            src_ref=mine(total, owner),
            dst_ref=mine(total, owner),
            send_sem=total_send_sem.at[o],
            recv_sem=total_recv_sem.at[o],
            device_id=(lat, lax.rem(col + o, n_col)),
            device_id_type=MESH,
        )

    def each(count, act):
        def body(o, carry):
            act(o)
            return carry

        lax.fori_loop(1, count, body, 0)

    each(n_col, lambda o: part_copy(o).start())
    here = pl.ds(pl.multiple_of(col * rows, 8), rows)

    def add_part(o, acc):
        part_copy(o).wait_recv()
        return acc + part_recv[o]

    lat_part[0] = lax.fori_loop(1, n_col, add_part, part[here, :])
    each(n_lat, lambda o: lat_copy(o).start())

    def add_lat(o, acc):
        lat_copy(o).wait_recv()
        return acc + lat_part[o]

    total[here, :] = lax.fori_loop(1, n_lat, add_lat, lat_part[0])
    each(n_col, lambda o: total_copy(o, col).start())
    each(n_col, lambda o: total_copy(o, lax.rem(col + n_col - o, n_col)).wait_recv())
    stores = (
        pltpu.make_async_copy(total, total_out, store_sem.at[1]),
        pltpu.make_async_copy(observed_out, observed_store, store_sem.at[2]),
    )
    for copy in stores:
        copy.start()

    each(n_col, lambda o: part_copy(o).wait_send())
    each(n_lat, lambda o: lat_copy(o).wait_send())
    each(n_col, lambda o: total_copy(o, col).wait_send())
    for t in range(steps):
        each(n_col, lambda o: slot_copy(t, o).wait_send())
        for side in range(4):

            @pl.when(exists[side])
            def _():
                halo(t, side).wait_send()

    store.wait()
    for copy in stores:
        copy.wait()


def split(x):
    high = x.astype(jnp.bfloat16)
    return high, (x - high.astype(jnp.float32)).astype(jnp.bfloat16)


def transform_kernel(final, observed, total, final_out, observed_out, values, results, gram, square, load_sem, store_sem):
    cells, m = final.shape
    watched = observed.shape[0]
    f32 = jnp.float32
    load_gram = pltpu.make_async_copy(total, gram, load_sem.at[0])
    load_final = pltpu.make_async_copy(final, values.at[pl.ds(0, cells)], load_sem.at[1])
    load_observed = pltpu.make_async_copy(observed, values.at[pl.ds(cells, watched)], load_sem.at[2])
    load_gram.start()
    load_observed.start()
    load_final.start()

    row, lane = (lax.broadcasted_iota(jnp.int32, (m, m), axis) for axis in (0, 1))
    identity = jnp.where(row == lane, 1.0, 0.0).astype(f32)
    load_gram.wait()
    square[:, 0:m] = gram[0:m, :] + identity
    square[:, m:] = identity
    line = lax.broadcasted_iota(jnp.int32, (8, m), 0)
    for low in range(0, m, 8):
        left, right = square[low : low + 8, 0:m], square[low : low + 8, m:]
        pivots = [jnp.broadcast_to(left[:, low + k : low + k + 1], (8, m)) for k in range(8)]

        def spread(x, j):
            return jnp.broadcast_to(x[j : j + 1, :], (8, m))

        for j in range(8):
            pivot = spread(pivots[j], j)
            root = lax.rsqrt(pivot)
            root = root * (1.5 - 0.5 * pivot * root * root)
            column = jnp.where(line > j, pivots[j] * root, 0.0)
            here = line == j
            x, y = spread(left, j) * root, spread(right, j) * root
            left = jnp.where(here, x, left - column * x)
            right = jnp.where(here, y, right - column * y)
            for k in range(j + 1, 8):
                pivots[k] = pivots[k] - column * spread(column, k)
        square[low : low + 8, m:] = right
        if low + 8 < m:
            both = jnp.concatenate([left, right], axis=1)
            a = both.astype(jnp.bfloat16).astype(f32)
            b = (both - a).astype(jnp.bfloat16).astype(f32)
            c = (both - a) - b
            one = jnp.concatenate([t[:, 0:m] for t in (a, a, b, b, a, c)], axis=0)
            two = jnp.concatenate([a, b, a, b, c, a], axis=0)
            update = jnp.dot(
                jnp.transpose(one).astype(jnp.bfloat16), two.astype(jnp.bfloat16), preferred_element_type=f32
            )
            square[low + 8 :, :] = square[low + 8 :, :] - update[low + 8 :, :]
    inverse = square[:, m:]
    push = gram[m : m + 1, :]
    inner = jnp.sum(inverse * push, axis=1, keepdims=True)
    offset = jnp.sum(inverse * inner, axis=0, keepdims=True) / math.sqrt(m - 1.0)
    turned = inverse + offset
    turned = turned - jnp.mean(turned, axis=1, keepdims=True) + 1.0 / m
    high, low = split(jnp.transpose(turned))
    line = jnp.concatenate([high, low], axis=1)
    mix = jnp.concatenate([line, line], axis=0)

    def apply(at, size):
        high, low = split(values[pl.ds(at, size), :])
        both = jnp.dot(jnp.concatenate([high, low], axis=1), mix, preferred_element_type=f32)
        results[pl.ds(at, size), :] = both[:, 0:m] + both[:, m:]

    tile = cells // 16
    load_final.wait()
    load_observed.wait()

    def store(q):
        here = pl.ds(pl.multiple_of(q * tile, 8), tile)
        return pltpu.make_async_copy(results.at[here], final_out.at[here], store_sem.at[q])

    def one_tile(q, carry):
        apply(pl.multiple_of(q * tile, 8), tile)
        store(q).start()
        return carry

    apply(cells, watched)
    store_observed = pltpu.make_async_copy(results.at[pl.ds(cells, watched)], observed_out, store_sem.at[16])
    store_observed.start()
    lax.fori_loop(0, 16, one_tile, 0)
    store_observed.wait()

    def finish(q, carry):
        store(q).wait()
        return carry

    lax.fori_loop(0, 16, finish, 0)


def on_device(
    n_lat,
    n_col,
    control,
    perturbations,
    zonal_flow,
    meridional_flow,
    diffusivity,
    send_cell,
    send_station,
    send_weight,
    send_count,
    obs_value,
    obs_error,
):
    nx, ny, m = perturbations.shape
    cap = send_cell.shape[3]
    steps, owned = obs_value.shape
    rows = slice_rows(m, n_col)
    f32 = jnp.float32
    state = pltpu.VMEM((nx + 2, ny + 2 * PAD, m), f32)
    dma = pltpu.SemaphoreType.DMA
    anywhere = pl.BlockSpec(memory_space=pl.ANY)
    final, observed, total = pl.pallas_call(
        functools.partial(forecast_kernel, n_lat, n_col),
        out_shape=(
            jax.ShapeDtypeStruct((nx, ny, m), f32),
            jax.ShapeDtypeStruct((steps, owned, m), f32),
            jax.ShapeDtypeStruct((n_col * rows, m), f32),
        ),
        in_specs=[anywhere] * 11,
        out_specs=(anywhere,) * 3,
        scratch_shapes=[
            pltpu.VMEM((nx, ny), f32),
            pltpu.VMEM((nx, ny), f32),
            pltpu.VMEM((nx, ny), f32),
            pltpu.VMEM((nx, ny), f32),
            pltpu.SMEM((n_col, cap), jnp.int32),
            pltpu.VMEM((n_col, cap), jnp.int32),
            pltpu.VMEM((n_col, cap), f32),
            pltpu.SMEM((1, n_col), jnp.int32),
            pltpu.VMEM((steps, owned), f32),
            pltpu.VMEM((steps, owned), f32),
            pltpu.VMEM((steps, owned, m), f32),
            pltpu.VMEM((4, nx, ny, m), f32),
            state,
            state,
            state,
            pltpu.VMEM((ny, 128), f32),
            pltpu.VMEM((ny, 128), f32),
            pltpu.VMEM((steps, 2, nx, m), f32),
            pltpu.VMEM((steps, 2, nx, m), f32),
            pltpu.VMEM((steps, 2, ny, m), f32),
            pltpu.VMEM((steps, n_col, cap + 8, m), f32),
            pltpu.VMEM((steps, n_col, cap + 8, m), f32),
            pltpu.VMEM((n_col * rows, m), f32),
            pltpu.VMEM((n_col, rows, m), f32),
            pltpu.VMEM((n_lat, rows, m), f32),
            pltpu.VMEM((n_col * rows, m), f32),
            dma((10,)),
            dma((4,)),
            dma((3,)),
            dma((steps, 4)),
            dma((steps, 4)),
            dma((steps, n_col)),
            dma((steps, n_col)),
            dma((n_col,)),
            dma((n_col,)),
            dma((n_lat,)),
            dma((n_lat,)),
            dma((n_col,)),
            dma((n_col,)),
        ],
        compiler_params=pltpu.CompilerParams(
            collective_id=0, has_side_effects=True, vmem_limit_bytes=56 * 1024 * 1024
        ),
    )(
        control,
        perturbations,
        zonal_flow,
        meridional_flow,
        diffusivity,
        send_cell[0, 0],
        send_station[0, 0],
        send_weight[0, 0],
        send_count[0],
        obs_value,
        obs_error,
    )
    cells, watched = nx * ny, steps * owned
    analysis, obs_analysis = pl.pallas_call(
        transform_kernel,
        out_shape=(jax.ShapeDtypeStruct((cells, m), f32), jax.ShapeDtypeStruct((watched, m), f32)),
        in_specs=[anywhere] * 3,
        out_specs=(anywhere,) * 2,
        scratch_shapes=[
            pltpu.VMEM((cells + watched, m), f32),
            pltpu.VMEM((cells + watched, m), f32),
            pltpu.VMEM(total.shape, f32),
            pltpu.VMEM((m, 2 * m), f32),
            dma((3,)),
            dma((17,)),
        ],
        compiler_params=pltpu.CompilerParams(vmem_limit_bytes=32 * 1024 * 1024),
    )(final.reshape(cells, m), observed.reshape(watched, m), total)
    return analysis.reshape(nx, ny, m), obs_analysis.reshape(steps, owned, m)


def solution(mesh):
    n_lat, n_col = mesh.shape["lat"], mesh.shape["col"]
    return jax.shard_map(
        functools.partial(on_device, n_lat, n_col),
        mesh=mesh,
        in_specs=(
            P("lat", "col"),
            P("lat", "col", None),
            P("lat", "col"),
            P("lat", "col"),
            P("lat", "col"),
            P("lat", "col", None, None),
            P("lat", "col", None, None),
            P("lat", "col", None, None),
            P("lat", "col", None),
            P(None, ("lat", "col")),
            P(None, ("lat", "col")),
        ),
        out_specs=(P("lat", "col", None), P(None, ("lat", "col"), None)),
        check_vma=False,
    )
```

```python
import functools
import math

import jax
import jax.numpy as jnp
from jax import lax
from jax.experimental import pallas as pl
from jax.experimental.pallas import tpu as pltpu
from jax.sharding import PartitionSpec as P

MESH = pl.DeviceIdType.MESH
exact_mode = lax.Precision.HIGHEST
PAD = 8


def slice_rows(members, count):
    return -(-(members + 1) // (8 * count)) * 8


def forecast_kernel(
    n_lat,
    n_col,
    control_in,
    perturbations,
    zonal_in,
    meridional_in,
    diffusion_in,
    cell_in,
    station_in,
    weight_in,
    live_in,
    obs_value_in,
    obs_error_in,
    final_out,
    observed_store,
    total_out,
    control,
    zonal,
    meridional,
    diffusion,
    cell,
    station,
    weight,
    live,
    obs_value,
    obs_error,
    observed_out,
    wide,
    state_0,
    state_1,
    state_2,
    rates,
    columns,
    edge_send,
    edge_recv,
    side_recv,
    slots_send,
    slots_recv,
    table_send,
    table_recv,
    part,
    part_recv,
    lat_part,
    total,
    small_sem,
    load_sem,
    store_sem,
    halo_send_sem,
    halo_recv_sem,
    slots_send_sem,
    slots_recv_sem,
    table_send_sem,
    table_recv_sem,
    part_send_sem,
    part_recv_sem,
    lat_send_sem,
    lat_recv_sem,
    total_send_sem,
    total_recv_sem,
):
    lat, col = lax.axis_index("lat"), lax.axis_index("col")
    nx, ny = control.shape
    m = perturbations.shape[2]
    cap = cell.shape[1]
    steps, owned = obs_value.shape
    states = (state_0, state_1, state_2)

    chunk = nx // 4
    loads = [
        pltpu.make_async_copy(
            perturbations.at[pl.ds(q * chunk, chunk)],
            state_0.at[pl.ds(1 + q * chunk, chunk), pl.ds(PAD, ny)],
            load_sem.at[q],
        )
        for q in range(4)
    ]
    pairs = (
        (zonal_in, zonal),
        (meridional_in, meridional),
        (diffusion_in, diffusion),
        (control_in, control),
        (obs_value_in, obs_value),
        (obs_error_in, obs_error),
        (cell_in, cell),
        (live_in, live),
        (station_in, station),
        (weight_in, weight),
    )
    smalls = [pltpu.make_async_copy(a, b, small_sem.at[q]) for q, (a, b) in enumerate(pairs)]
    for copy in smalls:
        copy.start()
    for q in (0, 3, 1, 2):
        loads[q].start()

    barrier = pltpu.get_barrier_semaphore()

    def greet_col(o, carry):
        pl.semaphore_signal(barrier, inc=1, device_id=(lat, lax.rem(col + o, n_col)), device_id_type=MESH)
        return carry

    def greet_lat(o, carry):
        pl.semaphore_signal(barrier, inc=1, device_id=(lax.rem(lat + o, n_lat), col), device_id_type=MESH)
        return carry

    lax.fori_loop(1, n_col, greet_col, 0)
    lax.fori_loop(1, n_lat, greet_lat, 0)

    for copy in smalls:
        copy.wait()
    u, v, d = zonal[...], meridional[...], diffusion[...]
    fields = [
        d + jnp.maximum(-u, 0.0),
        d + jnp.maximum(u, 0.0),
        d + jnp.maximum(-v, 0.0),
        d + jnp.maximum(v, 0.0),
    ]
    rates[...] = jnp.transpose(jnp.concatenate(fields, axis=0))
    rest = jnp.zeros((128 - nx - 2 * steps, ny), jnp.float32)
    columns[...] = jnp.transpose(jnp.concatenate([control[...], obs_value[...], obs_error[...], rest], axis=0))

    def widen(i, carry):
        shift = lax.rem(128 - i, 128)
        for j in range(0, ny, 64):
            k = pltpu.roll(rates[j : j + 64, :], shift, 1)
            for q in range(4):
                wide[q, i, j : j + 64, :] = jnp.broadcast_to(k[:, q * nx : q * nx + 1], (64, m))
        return carry

    def add_row(i, carry):
        shift = lax.rem(128 - i, 128)
        for j in range(0, ny, 64):
            centre = pltpu.roll(columns[j : j + 64, :], shift, 1)[:, 0:1]
            value = state_0[1 + i, PAD + j : PAD + j + 64, :] + centre
            state_0[1 + i, PAD + j : PAD + j + 64, :] = value
            if j == 0:
                edge_send[0, 0, pl.ds(i, 1), :] = value[0:1]
            if j == ny - 64:
                edge_send[0, 1, pl.ds(i, 1), :] = value[63:64]
        return carry

    def halo(t, side):
        source = states[t]
        if side == 0:
            src, dst, to = source.at[1, pl.ds(PAD, ny)], side_recv.at[t, 1], (lat - 1, col)
        elif side == 1:
            src, dst, to = source.at[nx, pl.ds(PAD, ny)], side_recv.at[t, 0], (lat + 1, col)
        elif side == 2:
            src, dst, to = edge_send.at[t, 0], edge_recv.at[t, 1], (lat, col - 1)
        else:
            src, dst, to = edge_send.at[t, 1], edge_recv.at[t, 0], (lat, col + 1)
        arrives = side ^ 1
        send = pltpu.make_async_remote_copy(
            src_ref=src,
            dst_ref=dst,
            send_sem=halo_send_sem.at[t, side],
            recv_sem=halo_recv_sem.at[t, arrives],
            device_id=to,
            device_id_type=MESH,
        )
        return send

    exists = (lat > 0, lat < n_lat - 1, col > 0, col < n_col - 1)

    def send_halo(t, side):
        @pl.when(exists[side])
        def _():
            halo(t, side).start()

    def take_halo(t, side):
        target = states[t]

        @pl.when(exists[side])
        def _():
            halo(t, side ^ 1).wait_recv()
            if side < 2:
                target[(nx + 1) * side, PAD : PAD + ny, :] = side_recv[t, side]
            else:
                at = PAD - 1 if side == 2 else PAD + ny

                def put(i, carry):
                    target[1 + i, at : at + 1, :] = edge_recv[t, side - 2, pl.ds(i, 1), :]
                    return carry

                lax.fori_loop(0, nx, put, 0)

        @pl.when(jnp.logical_not(exists[side]))
        def _():
            if side < 2:
                target[(nx + 1) * side, PAD : PAD + ny, :] = jnp.zeros((ny, m), jnp.float32)
            else:
                at = PAD - 1 if side == 2 else PAD + ny

                def put(i, carry):
                    target[1 + i, at : at + 1, :] = jnp.zeros((1, m), jnp.float32)
                    return carry

                lax.fori_loop(0, nx, put, 0)

    def step_row(t, i, carry):
        source, target = states[t], states[t + 1]
        for j in range(0, ny, 64):
            k = [wide[q, i, j : j + 64, :] for q in range(4)]
            at = PAD + j
            centre = source[1 + i, at : at + 64, :]
            value = centre + k[0] * (source[2 + i, at : at + 64, :] - centre)
            value = value + k[1] * (source[i, at : at + 64, :] - centre)
            value = value + k[2] * (source[1 + i, at + 1 : at + 65, :] - centre)
            value = value + k[3] * (source[1 + i, at - 1 : at + 63, :] - centre)
            target[1 + i, at : at + 64, :] = value
            if t + 1 < steps:
                if j == 0:
                    edge_send[t + 1, 0, pl.ds(i, 1), :] = value[0:1]
                if j == ny - 64:
                    edge_send[t + 1, 1, pl.ds(i, 1), :] = value[63:64]
        return carry

    half = n_col // 2
    side_of, place = lax.div(col, half), lax.rem(col, half)
    mirror = (1 - side_of) * half + place

    def peer(k):
        return side_of * half + lax.rem(place + k, half)

    def slot_copy(t, kind, k):
        rows = cap + 8 if t == 0 else cap
        return pltpu.make_async_remote_copy(
            src_ref=slots_send.at[t, kind, k, pl.ds(0, rows)],
            dst_ref=slots_recv.at[t, kind, k, pl.ds(0, rows)],
            send_sem=slots_send_sem.at[t, kind, k],
            recv_sem=slots_recv_sem.at[t, kind, k],
            device_id=(lat, peer(k)),
            device_id_type=MESH,
        )

    def table_copy(t):
        return pltpu.make_async_remote_copy(
            src_ref=table_send.at[t],
            dst_ref=table_recv.at[t],
            send_sem=table_send_sem.at[t],
            recv_sem=table_recv_sem.at[t],
            device_id=(lat, mirror),
            device_id_type=MESH,
        )

    bits = ny.bit_length() - 1

    def fill(t, kind, k):
        source = states[t + 1]
        receiver = (1 - side_of if kind == 0 else side_of) * half + lax.rem(place + k, half)

        def group(g, carry):
            for r in range(16):
                c = cell[receiver, g * 16 + r]
                i, j = lax.shift_right_logical(c, bits), c & (ny - 1)
                slots_send[t, kind, k, pl.ds(g * 16 + r, 1), :] = source[1 + i, pl.ds(PAD + j, 1), :]
            return carry

        lax.fori_loop(0, cap // 16, group, 0)
        if t == 0:
            lane = lax.broadcasted_iota(jnp.int32, (1, cap), 1)
            factor = jnp.where(lane < live[0, receiver], weight[pl.ds(receiver, 1), :], 0.0)
            line = lax.broadcasted_iota(jnp.int32, (8, cap), 0)
            head = jnp.where(line == 0, station[pl.ds(receiver, 1), :].astype(jnp.float32), factor)
            slots_send[t, kind, k, pl.ds(cap, 8), :] = head

    def send_slots(t, kind):
        def one(k, carry):
            fill(t, kind, k)
            slot_copy(t, kind, k).start()
            return carry

        lax.fori_loop(1, half, one, 0)
        fill(t, kind, 0)

    def gather_sum(t, kind, target):
        line = lax.broadcasted_iota(jnp.int32, (owned, cap), 0).astype(jnp.float32)

        def product(head, values):
            mix = jnp.where(line == head[0:1], head[1:2], 0.0)
            return jnp.dot(mix, values, precision=exact_mode, preferred_element_type=jnp.float32)

        target[t] = product(slots_send[0, kind, 0, pl.ds(cap, 8), :], slots_send[t, kind, 0, pl.ds(0, cap), :])

        def one(k, carry):
            slot_copy(t, kind, k).wait_recv()
            target[t] += product(slots_recv[0, kind, k, pl.ds(cap, 8), :], slots_recv[t, kind, k, pl.ds(0, cap), :])
            return carry

        lax.fori_loop(1, half, one, 0)

    def send_table(t):
        gather_sum(t, 0, table_send)
        table_copy(t).start()

    loads[0].wait()
    loads[3].wait()
    add_row(0, 0)
    add_row(nx - 1, 0)
    pl.semaphore_wait(barrier, n_col + n_lat - 2)
    send_halo(0, 0)
    send_halo(0, 1)
    loads[1].wait()
    loads[2].wait()
    lax.fori_loop(1, nx - 1, add_row, 0)
    send_halo(0, 2)
    send_halo(0, 3)
    lax.fori_loop(0, nx, widen, 0)

    for t in range(steps):
        take_halo(t, 2)
        take_halo(t, 3)
        lax.fori_loop(1, nx - 1, functools.partial(step_row, t), 0)
        take_halo(t, 0)
        take_halo(t, 1)
        step_row(t, 0, 0)
        step_row(t, nx - 1, 0)
        if t + 1 < steps:
            for side in range(4):
                send_halo(t + 1, side)
        if t > 0:
            send_table(t - 1)
        send_slots(t, 0)
        send_slots(t, 1)
    store = pltpu.make_async_copy(state_2.at[pl.ds(1, nx), pl.ds(PAD, ny)], final_out, store_sem.at[0])
    store.start()

    send_table(steps - 1)
    for t in range(steps):
        gather_sum(t, 1, observed_out)

    root_scale = math.sqrt(m - 1.0)
    part[...] = jnp.zeros_like(part)
    gram = jnp.zeros((m, m), jnp.float32)
    push = jnp.zeros((1, m), jnp.float32)
    for t in range(steps):
        table_copy(t).wait_recv()
        observed_out[t] += table_recv[t]
        observed = observed_out[t]
        mean = jnp.mean(observed, axis=1, keepdims=True)
        spread = observed - mean
        error = columns[:, nx + steps + t : nx + steps + t + 1]
        scaled = spread / (error * root_scale)
        innovation = (columns[:, nx + t : nx + t + 1] - mean) / error
        gram = gram + lax.dot_general(
            scaled, scaled, (((0,), (0,)), ((), ())), precision=exact_mode, preferred_element_type=jnp.float32
        )
        push = push + jnp.sum(scaled * innovation, axis=0, keepdims=True)
    part[0:m, :] = gram
    part[m : m + 1, :] = push

    rows = part_recv.shape[1]

    def mine(ref, who):
        return ref.at[pl.ds(pl.multiple_of(who * rows, 8), rows)]

    def part_copy(o):
        who = lax.rem(col + o, n_col)
        return pltpu.make_async_remote_copy(
            src_ref=mine(part, who),
            dst_ref=part_recv.at[o],
            send_sem=part_send_sem.at[o],
            recv_sem=part_recv_sem.at[o],
            device_id=(lat, who),
            device_id_type=MESH,
        )

    def lat_copy(o):
        return pltpu.make_async_remote_copy(
            src_ref=lat_part.at[0],
            dst_ref=lat_part.at[o],
            send_sem=lat_send_sem.at[o],
            recv_sem=lat_recv_sem.at[o],
            device_id=(lax.rem(lat + o, n_lat), col),
            device_id_type=MESH,
        )

    def total_copy(o, owner):
        return pltpu.make_async_remote_copy(
            src_ref=mine(total, owner),
            dst_ref=mine(total, owner),
            send_sem=total_send_sem.at[o],
            recv_sem=total_recv_sem.at[o],
            device_id=(lat, lax.rem(col + o, n_col)),
            device_id_type=MESH,
        )

    def each(count, act):
        def body(o, carry):
            act(o)
            return carry

        lax.fori_loop(1, count, body, 0)

    each(n_col, lambda o: part_copy(o).start())
    here = pl.ds(pl.multiple_of(col * rows, 8), rows)

    def add_part(o, acc):
        part_copy(o).wait_recv()
        return acc + part_recv[o]

    lat_part[0] = lax.fori_loop(1, n_col, add_part, part[here, :])
    each(n_lat, lambda o: lat_copy(o).start())

    def add_lat(o, acc):
        lat_copy(o).wait_recv()
        return acc + lat_part[o]

    total[here, :] = lax.fori_loop(1, n_lat, add_lat, lat_part[0])
    each(n_col, lambda o: total_copy(o, col).start())
    each(n_col, lambda o: total_copy(o, lax.rem(col + n_col - o, n_col)).wait_recv())
    stores = (
        pltpu.make_async_copy(total, total_out, store_sem.at[1]),
        pltpu.make_async_copy(observed_out, observed_store, store_sem.at[2]),
    )
    for copy in stores:
        copy.start()

    each(n_col, lambda o: part_copy(o).wait_send())
    each(n_lat, lambda o: lat_copy(o).wait_send())
    each(n_col, lambda o: total_copy(o, col).wait_send())
    for t in range(steps):
        each(half, lambda k: slot_copy(t, 0, k).wait_send())
        each(half, lambda k: slot_copy(t, 1, k).wait_send())
        table_copy(t).wait_send()
        for side in range(4):

            @pl.when(exists[side])
            def _():
                halo(t, side).wait_send()

    store.wait()
    for copy in stores:
        copy.wait()


def split(x):
    high = x.astype(jnp.bfloat16)
    return high, (x - high.astype(jnp.float32)).astype(jnp.bfloat16)


def transform_kernel(final, observed, total, final_out, observed_out, values, results, gram, square, load_sem, store_sem):
    cells, m = final.shape
    watched = observed.shape[0]
    f32 = jnp.float32
    load_gram = pltpu.make_async_copy(total, gram, load_sem.at[0])
    load_final = pltpu.make_async_copy(final, values.at[pl.ds(0, cells)], load_sem.at[1])
    load_observed = pltpu.make_async_copy(observed, values.at[pl.ds(cells, watched)], load_sem.at[2])
    load_gram.start()
    load_observed.start()
    load_final.start()

    row, lane = (lax.broadcasted_iota(jnp.int32, (m, m), axis) for axis in (0, 1))
    identity = jnp.where(row == lane, 1.0, 0.0).astype(f32)
    load_gram.wait()
    square[:, 0:m] = gram[0:m, :] + identity
    square[:, m:] = identity
    line = lax.broadcasted_iota(jnp.int32, (8, m), 0)
    for low in range(0, m, 8):
        left, right = square[low : low + 8, 0:m], square[low : low + 8, m:]
        pivots = [jnp.broadcast_to(left[:, low + k : low + k + 1], (8, m)) for k in range(8)]

        def spread(x, j):
            return jnp.broadcast_to(x[j : j + 1, :], (8, m))

        for j in range(8):
            pivot = spread(pivots[j], j)
            root = lax.rsqrt(pivot)
            root = root * (1.5 - 0.5 * pivot * root * root)
            column = jnp.where(line > j, pivots[j] * root, 0.0)
            here = line == j
            x, y = spread(left, j) * root, spread(right, j) * root
            left = jnp.where(here, x, left - column * x)
            right = jnp.where(here, y, right - column * y)
            for k in range(j + 1, 8):
                pivots[k] = pivots[k] - column * spread(column, k)
        square[low : low + 8, m:] = right
        if low + 8 < m:
            both = jnp.concatenate([left, right], axis=1)
            a = both.astype(jnp.bfloat16).astype(f32)
            b = (both - a).astype(jnp.bfloat16).astype(f32)
            c = (both - a) - b
            one = jnp.concatenate([t[:, 0:m] for t in (a, a, b, b, a, c)], axis=0)
            two = jnp.concatenate([a, b, a, b, c, a], axis=0)
            update = jnp.dot(
                jnp.transpose(one).astype(jnp.bfloat16), two.astype(jnp.bfloat16), preferred_element_type=f32
            )
            square[low + 8 :, :] = square[low + 8 :, :] - update[low + 8 :, :]
    inverse = square[:, m:]
    push = gram[m : m + 1, :]
    inner = jnp.sum(inverse * push, axis=1, keepdims=True)
    offset = jnp.sum(inverse * inner, axis=0, keepdims=True) / math.sqrt(m - 1.0)
    turned = inverse + offset
    turned = turned - jnp.mean(turned, axis=1, keepdims=True) + 1.0 / m
    high, low = split(jnp.transpose(turned))
    line = jnp.concatenate([high, low], axis=1)
    mix = jnp.concatenate([line, line], axis=0)

    def apply(at, size):
        high, low = split(values[pl.ds(at, size), :])
        both = jnp.dot(jnp.concatenate([high, low], axis=1), mix, preferred_element_type=f32)
        results[pl.ds(at, size), :] = both[:, 0:m] + both[:, m:]

    tile = cells // 16
    load_final.wait()
    load_observed.wait()

    def store(q):
        here = pl.ds(pl.multiple_of(q * tile, 8), tile)
        return pltpu.make_async_copy(results.at[here], final_out.at[here], store_sem.at[q])

    def one_tile(q, carry):
        apply(pl.multiple_of(q * tile, 8), tile)
        store(q).start()
        return carry

    apply(cells, watched)
    store_observed = pltpu.make_async_copy(results.at[pl.ds(cells, watched)], observed_out, store_sem.at[16])
    store_observed.start()
    lax.fori_loop(0, 16, one_tile, 0)
    store_observed.wait()

    def finish(q, carry):
        store(q).wait()
        return carry

    lax.fori_loop(0, 16, finish, 0)


def on_device(
    n_lat,
    n_col,
    control,
    perturbations,
    zonal_flow,
    meridional_flow,
    diffusivity,
    send_cell,
    send_station,
    send_weight,
    send_count,
    obs_value,
    obs_error,
):
    nx, ny, m = perturbations.shape
    cap = send_cell.shape[3]
    steps, owned = obs_value.shape
    rows = slice_rows(m, n_col)
    f32 = jnp.float32
    state = pltpu.VMEM((nx + 2, ny + 2 * PAD, m), f32)
    dma = pltpu.SemaphoreType.DMA
    anywhere = pl.BlockSpec(memory_space=pl.ANY)
    final, observed, total = pl.pallas_call(
        functools.partial(forecast_kernel, n_lat, n_col),
        out_shape=(
            jax.ShapeDtypeStruct((nx, ny, m), f32),
            jax.ShapeDtypeStruct((steps, owned, m), f32),
            jax.ShapeDtypeStruct((n_col * rows, m), f32),
        ),
        in_specs=[anywhere] * 11,
        out_specs=(anywhere,) * 3,
        scratch_shapes=[
            pltpu.VMEM((nx, ny), f32),
            pltpu.VMEM((nx, ny), f32),
            pltpu.VMEM((nx, ny), f32),
            pltpu.VMEM((nx, ny), f32),
            pltpu.SMEM((n_col, cap), jnp.int32),
            pltpu.VMEM((n_col, cap), jnp.int32),
            pltpu.VMEM((n_col, cap), f32),
            pltpu.SMEM((1, n_col), jnp.int32),
            pltpu.VMEM((steps, owned), f32),
            pltpu.VMEM((steps, owned), f32),
            pltpu.VMEM((steps, owned, m), f32),
            pltpu.VMEM((4, nx, ny, m), f32),
            state,
            state,
            state,
            pltpu.VMEM((ny, 128), f32),
            pltpu.VMEM((ny, 128), f32),
            pltpu.VMEM((steps, 2, nx, m), f32),
            pltpu.VMEM((steps, 2, nx, m), f32),
            pltpu.VMEM((steps, 2, ny, m), f32),
            pltpu.VMEM((steps, 2, n_col // 2, cap + 8, m), f32),
            pltpu.VMEM((steps, 2, n_col // 2, cap + 8, m), f32),
            pltpu.VMEM((steps, owned, m), f32),
            pltpu.VMEM((steps, owned, m), f32),
            pltpu.VMEM((n_col * rows, m), f32),
            pltpu.VMEM((n_col, rows, m), f32),
            pltpu.VMEM((n_lat, rows, m), f32),
            pltpu.VMEM((n_col * rows, m), f32),
            dma((10,)),
            dma((4,)),
            dma((3,)),
            dma((steps, 4)),
            dma((steps, 4)),
            dma((steps, 2, n_col // 2)),
            dma((steps, 2, n_col // 2)),
            dma((steps,)),
            dma((steps,)),
            dma((n_col,)),
            dma((n_col,)),
            dma((n_lat,)),
            dma((n_lat,)),
            dma((n_col,)),
            dma((n_col,)),
        ],
        compiler_params=pltpu.CompilerParams(
            collective_id=0, has_side_effects=True, vmem_limit_bytes=56 * 1024 * 1024
        ),
    )(
        control,
        perturbations,
        zonal_flow,
        meridional_flow,
        diffusivity,
        send_cell[0, 0],
        send_station[0, 0],
        send_weight[0, 0],
        send_count[0],
        obs_value,
        obs_error,
    )
    cells, watched = nx * ny, steps * owned
    analysis, obs_analysis = pl.pallas_call(
        transform_kernel,
        out_shape=(jax.ShapeDtypeStruct((cells, m), f32), jax.ShapeDtypeStruct((watched, m), f32)),
        in_specs=[anywhere] * 3,
        out_specs=(anywhere,) * 2,
        scratch_shapes=[
            pltpu.VMEM((cells + watched, m), f32),
            pltpu.VMEM((cells + watched, m), f32),
            pltpu.VMEM(total.shape, f32),
            pltpu.VMEM((m, 2 * m), f32),
            dma((3,)),
            dma((17,)),
        ],
        compiler_params=pltpu.CompilerParams(vmem_limit_bytes=60 * 1024 * 1024),
    )(final.reshape(cells, m), observed.reshape(watched, m), total)
    return analysis.reshape(nx, ny, m), obs_analysis.reshape(steps, owned, m)


def solution(mesh):
    n_lat, n_col = mesh.shape["lat"], mesh.shape["col"]
    return jax.shard_map(
        functools.partial(on_device, n_lat, n_col),
        mesh=mesh,
        in_specs=(
            P("lat", "col"),
            P("lat", "col", None),
            P("lat", "col"),
            P("lat", "col"),
            P("lat", "col"),
            P("lat", "col", None, None),
            P("lat", "col", None, None),
            P("lat", "col", None, None),
            P("lat", "col", None),
            P(None, ("lat", "col")),
            P(None, ("lat", "col")),
        ),
        out_specs=(P("lat", "col", None), P(None, ("lat", "col"), None)),
        check_vma=False,
    )
```

```python
import functools
import math

import jax
import jax.numpy as jnp
from jax import lax
from jax.experimental import pallas as pl
from jax.experimental.pallas import tpu as pltpu
from jax.sharding import PartitionSpec as P

MESH = pl.DeviceIdType.MESH
exact_mode = lax.Precision.HIGHEST
PAD = 8


def slice_rows(members, count):
    return -(-(members + 1) // (8 * count)) * 8


def thirds(x):
    high = x.astype(jnp.bfloat16)
    rest = x - high.astype(jnp.float32)
    middle = rest.astype(jnp.bfloat16)
    return high, middle, (rest - middle.astype(jnp.float32)).astype(jnp.bfloat16)


def forecast_kernel(
    n_lat,
    n_col,
    control_in,
    perturbations,
    zonal_in,
    meridional_in,
    diffusion_in,
    cell_in,
    station_in,
    weight_in,
    live_in,
    obs_value_in,
    obs_error_in,
    final_out,
    observed_store,
    total_out,
    control,
    zonal,
    meridional,
    diffusion,
    cell,
    station,
    weight,
    live,
    obs_value,
    obs_error,
    observed_out,
    wide,
    state_0,
    state_1,
    state_2,
    rates,
    columns,
    edge_send,
    edge_recv,
    side_recv,
    slots_send,
    slots_recv,
    table_send,
    table_recv,
    part,
    part_recv,
    lat_part,
    total,
    small_sem,
    load_sem,
    store_sem,
    halo_send_sem,
    halo_recv_sem,
    slots_send_sem,
    slots_recv_sem,
    table_send_sem,
    table_recv_sem,
    part_send_sem,
    part_recv_sem,
    lat_send_sem,
    lat_recv_sem,
    total_send_sem,
    total_recv_sem,
):
    lat, col = lax.axis_index("lat"), lax.axis_index("col")
    nx, ny = control.shape
    m = perturbations.shape[2]
    cap = cell.shape[1]
    steps, owned = obs_value.shape
    states = (state_0, state_1, state_2)

    chunk = nx // 4
    loads = [
        pltpu.make_async_copy(
            perturbations.at[pl.ds(q * chunk, chunk)],
            state_0.at[pl.ds(1 + q * chunk, chunk), pl.ds(PAD, ny)],
            load_sem.at[q],
        )
        for q in range(4)
    ]
    pairs = (
        (zonal_in, zonal),
        (meridional_in, meridional),
        (diffusion_in, diffusion),
        (control_in, control),
        (obs_value_in, obs_value),
        (obs_error_in, obs_error),
        (cell_in, cell),
        (live_in, live),
        (station_in, station),
        (weight_in, weight),
    )
    smalls = [pltpu.make_async_copy(a, b, small_sem.at[q]) for q, (a, b) in enumerate(pairs)]
    for copy in smalls:
        copy.start()
    for q in (0, 3, 1, 2):
        loads[q].start()

    barrier = pltpu.get_barrier_semaphore()

    def greet_col(o, carry):
        pl.semaphore_signal(barrier, inc=1, device_id=(lat, lax.rem(col + o, n_col)), device_id_type=MESH)
        return carry

    def greet_lat(o, carry):
        pl.semaphore_signal(barrier, inc=1, device_id=(lax.rem(lat + o, n_lat), col), device_id_type=MESH)
        return carry

    lax.fori_loop(1, n_col, greet_col, 0)
    lax.fori_loop(1, n_lat, greet_lat, 0)

    for copy in smalls:
        copy.wait()
    u, v, d = zonal[...], meridional[...], diffusion[...]
    fields = [
        d + jnp.maximum(-u, 0.0),
        d + jnp.maximum(u, 0.0),
        d + jnp.maximum(-v, 0.0),
        d + jnp.maximum(v, 0.0),
    ]
    rates[...] = jnp.transpose(jnp.concatenate(fields, axis=0))
    rest = jnp.zeros((128 - nx - 2 * steps, ny), jnp.float32)
    columns[...] = jnp.transpose(jnp.concatenate([control[...], obs_value[...], obs_error[...], rest], axis=0))

    def widen(i, carry):
        shift = lax.rem(128 - i, 128)
        for j in range(0, ny, 64):
            k = pltpu.roll(rates[j : j + 64, :], shift, 1)
            for q in range(4):
                wide[q, i, j : j + 64, :] = jnp.broadcast_to(k[:, q * nx : q * nx + 1], (64, m))
        return carry

    def add_row(i, carry):
        shift = lax.rem(128 - i, 128)
        for j in range(0, ny, 64):
            centre = pltpu.roll(columns[j : j + 64, :], shift, 1)[:, 0:1]
            value = state_0[1 + i, PAD + j : PAD + j + 64, :] + centre
            state_0[1 + i, PAD + j : PAD + j + 64, :] = value
            if j == 0:
                edge_send[0, 0, pl.ds(i, 1), :] = value[0:1]
            if j == ny - 64:
                edge_send[0, 1, pl.ds(i, 1), :] = value[63:64]
        return carry

    def halo(t, side):
        source = states[t]
        if side == 0:
            src, dst, to = source.at[1, pl.ds(PAD, ny)], side_recv.at[t, 1], (lat - 1, col)
        elif side == 1:
            src, dst, to = source.at[nx, pl.ds(PAD, ny)], side_recv.at[t, 0], (lat + 1, col)
        elif side == 2:
            src, dst, to = edge_send.at[t, 0], edge_recv.at[t, 1], (lat, col - 1)
        else:
            src, dst, to = edge_send.at[t, 1], edge_recv.at[t, 0], (lat, col + 1)
        arrives = side ^ 1
        send = pltpu.make_async_remote_copy(
            src_ref=src,
            dst_ref=dst,
            send_sem=halo_send_sem.at[t, side],
            recv_sem=halo_recv_sem.at[t, arrives],
            device_id=to,
            device_id_type=MESH,
        )
        return send

    exists = (lat > 0, lat < n_lat - 1, col > 0, col < n_col - 1)

    def send_halo(t, side):
        @pl.when(exists[side])
        def _():
            halo(t, side).start()

    def take_halo(t, side):
        target = states[t]

        @pl.when(exists[side])
        def _():
            halo(t, side ^ 1).wait_recv()
            if side < 2:
                target[(nx + 1) * side, PAD : PAD + ny, :] = side_recv[t, side]
            else:
                at = PAD - 1 if side == 2 else PAD + ny

                def put(g, carry):
                    taken = edge_recv[t, side - 2, pl.ds(pl.multiple_of(g * 8, 8), 8), :]
                    for r in range(8):
                        target[1 + g * 8 + r, at : at + 1, :] = taken[r : r + 1]
                    return carry

                lax.fori_loop(0, nx // 8, put, 0)

        @pl.when(jnp.logical_not(exists[side]))
        def _():
            if side < 2:
                target[(nx + 1) * side, PAD : PAD + ny, :] = jnp.zeros((ny, m), jnp.float32)
            else:
                at = PAD - 1 if side == 2 else PAD + ny

                def put(i, carry):
                    target[1 + i, at : at + 1, :] = jnp.zeros((1, m), jnp.float32)
                    return carry

                lax.fori_loop(0, nx, put, 0)

    def step_row(t, i, carry):
        source, target = states[t], states[t + 1]
        for j in range(0, ny, 64):
            k = [wide[q, i, j : j + 64, :] for q in range(4)]
            at = PAD + j
            centre = source[1 + i, at : at + 64, :]
            value = centre + k[0] * (source[2 + i, at : at + 64, :] - centre)
            value = value + k[1] * (source[i, at : at + 64, :] - centre)
            value = value + k[2] * (source[1 + i, at + 1 : at + 65, :] - centre)
            value = value + k[3] * (source[1 + i, at - 1 : at + 63, :] - centre)
            target[1 + i, at : at + 64, :] = value
            if t + 1 < steps:
                if j == 0:
                    edge_send[t + 1, 0, pl.ds(i, 1), :] = value[0:1]
                if j == ny - 64:
                    edge_send[t + 1, 1, pl.ds(i, 1), :] = value[63:64]
        return carry

    half = n_col // 2
    side_of, place = lax.div(col, half), lax.rem(col, half)
    mirror = (1 - side_of) * half + place

    def peer(k):
        return side_of * half + lax.rem(place + k, half)

    def slot_copy(t, kind, k):
        rows = cap + 8 if t == 0 else cap
        return pltpu.make_async_remote_copy(
            src_ref=slots_send.at[t, kind, k, pl.ds(0, rows)],
            dst_ref=slots_recv.at[t, kind, k, pl.ds(0, rows)],
            send_sem=slots_send_sem.at[t, kind, k],
            recv_sem=slots_recv_sem.at[t, kind, k],
            device_id=(lat, peer(k)),
            device_id_type=MESH,
        )

    def table_copy(t):
        return pltpu.make_async_remote_copy(
            src_ref=table_send.at[t],
            dst_ref=table_recv.at[t],
            send_sem=table_send_sem.at[t],
            recv_sem=table_recv_sem.at[t],
            device_id=(lat, mirror),
            device_id_type=MESH,
        )

    bits = ny.bit_length() - 1

    def fill(t, kind, k):
        source = states[t + 1]
        receiver = (1 - side_of if kind == 0 else side_of) * half + lax.rem(place + k, half)

        def group(g, carry):
            taken = []
            for r in range(16):
                c = cell[receiver, g * 16 + r]
                i, j = lax.shift_right_logical(c, bits), c & (ny - 1)
                taken.append(source[1 + i, pl.ds(PAD + j, 1), :])
            for r in range(16):
                slots_send[t, kind, k, pl.ds(g * 16 + r, 1), :] = taken[r]
            return carry

        lax.fori_loop(0, cap // 16, group, 0)
        if t == 0:
            lane = lax.broadcasted_iota(jnp.int32, (1, cap), 1)
            factor = jnp.where(lane < live[0, receiver], weight[pl.ds(receiver, 1), :], 0.0)
            line = lax.broadcasted_iota(jnp.int32, (8, cap), 0)
            head = jnp.where(line == 0, station[pl.ds(receiver, 1), :].astype(jnp.float32), factor)
            slots_send[t, kind, k, pl.ds(cap, 8), :] = head

    def send_slots(t, kind):
        def one(k, carry):
            fill(t, kind, k)
            slot_copy(t, kind, k).start()
            return carry

        lax.fori_loop(1, half, one, 0)
        fill(t, kind, 0)

    def gather_sum(t, kind, target):
        line = lax.broadcasted_iota(jnp.int32, (owned, cap), 0).astype(jnp.float32)

        def product(head, values):
            pick = jnp.where(line == head[0:1], 1.0, 0.0).astype(jnp.bfloat16)
            high, middle, low = thirds(values * jnp.transpose(head)[:, 1:2])
            upper = jnp.concatenate([high, low], axis=1)
            lower = jnp.concatenate([middle, jnp.zeros_like(middle)], axis=1)
            both = jnp.dot(
                jnp.concatenate([pick, pick], axis=1),
                jnp.concatenate([upper, lower], axis=0),
                preferred_element_type=jnp.float32,
            )
            return both[:, :m] + both[:, m:]

        target[t] = product(slots_send[0, kind, 0, pl.ds(cap, 8), :], slots_send[t, kind, 0, pl.ds(0, cap), :])

        def one(k, carry):
            slot_copy(t, kind, k).wait_recv()
            target[t] += product(slots_recv[0, kind, k, pl.ds(cap, 8), :], slots_recv[t, kind, k, pl.ds(0, cap), :])
            return carry

        lax.fori_loop(1, half, one, 0)

    def send_table(t):
        gather_sum(t, 0, table_send)
        table_copy(t).start()

    loads[0].wait()
    loads[3].wait()
    add_row(0, 0)
    add_row(nx - 1, 0)
    pl.semaphore_wait(barrier, n_col + n_lat - 2)
    send_halo(0, 0)
    send_halo(0, 1)
    loads[1].wait()
    loads[2].wait()
    lax.fori_loop(1, nx - 1, add_row, 0)
    send_halo(0, 2)
    send_halo(0, 3)
    lax.fori_loop(0, nx, widen, 0)

    for t in range(steps):
        take_halo(t, 2)
        take_halo(t, 3)
        lax.fori_loop(1, nx - 1, functools.partial(step_row, t), 0)
        take_halo(t, 0)
        take_halo(t, 1)
        step_row(t, 0, 0)
        step_row(t, nx - 1, 0)
        if t + 1 < steps:
            for side in range(4):
                send_halo(t + 1, side)
        if t > 0:
            send_table(t - 1)
        send_slots(t, 0)
        send_slots(t, 1)
    store = pltpu.make_async_copy(state_2.at[pl.ds(1, nx), pl.ds(PAD, ny)], final_out, store_sem.at[0])
    store.start()

    send_table(steps - 1)
    for t in range(steps):
        gather_sum(t, 1, observed_out)

    root_scale = math.sqrt(m - 1.0)
    part[...] = jnp.zeros_like(part)
    members = []
    push = jnp.zeros((1, m), jnp.float32)
    for t in range(steps):
        table_copy(t).wait_recv()
        observed_out[t] += table_recv[t]
        observed = observed_out[t]
        mean = jnp.mean(observed, axis=1, keepdims=True)
        spread = observed - mean
        error = columns[:, nx + steps + t : nx + steps + t + 1]
        scaled = spread / (error * root_scale)
        innovation = (columns[:, nx + t : nx + t + 1] - mean) / error
        members.append(scaled)
        push = push + jnp.sum(scaled * innovation, axis=0, keepdims=True)
    scaled = jnp.concatenate(members, axis=0)
    high, middle, low = thirds(scaled)
    turned = jnp.transpose(scaled)
    turned_high, turned_middle, _ = thirds(turned)
    products = jnp.dot(
        jnp.concatenate([turned_high, turned_middle], axis=0),
        jnp.concatenate([high, middle], axis=1),
        preferred_element_type=jnp.float32,
    )
    cross = jnp.dot(turned_high, low, preferred_element_type=jnp.float32)
    small = products[m:, m:] + cross + jnp.transpose(cross)
    part[0:m, :] = products[:m, :m] + (products[:m, m:] + products[m:, :m] + small)
    part[m : m + 1, :] = push

    rows = part_recv.shape[1]

    def mine(ref, who):
        return ref.at[pl.ds(pl.multiple_of(who * rows, 8), rows)]

    def part_copy(o):
        who = lax.rem(col + o, n_col)
        return pltpu.make_async_remote_copy(
            src_ref=mine(part, who),
            dst_ref=part_recv.at[o],
            send_sem=part_send_sem.at[o],
            recv_sem=part_recv_sem.at[o],
            device_id=(lat, who),
            device_id_type=MESH,
        )

    def lat_copy(o):
        return pltpu.make_async_remote_copy(
            src_ref=lat_part.at[0],
            dst_ref=lat_part.at[o],
            send_sem=lat_send_sem.at[o],
            recv_sem=lat_recv_sem.at[o],
            device_id=(lax.rem(lat + o, n_lat), col),
            device_id_type=MESH,
        )

    def total_copy(o, owner):
        return pltpu.make_async_remote_copy(
            src_ref=mine(total, owner),
            dst_ref=mine(total, owner),
            send_sem=total_send_sem.at[o],
            recv_sem=total_recv_sem.at[o],
            device_id=(lat, lax.rem(col + o, n_col)),
            device_id_type=MESH,
        )

    def each(count, act):
        def body(o, carry):
            act(o)
            return carry

        lax.fori_loop(1, count, body, 0)

    each(n_col, lambda o: part_copy(o).start())
    here = pl.ds(pl.multiple_of(col * rows, 8), rows)

    def add_part(o, acc):
        part_copy(o).wait_recv()
        return acc + part_recv[o]

    lat_part[0] = lax.fori_loop(1, n_col, add_part, part[here, :])
    each(n_lat, lambda o: lat_copy(o).start())

    def add_lat(o, acc):
        lat_copy(o).wait_recv()
        return acc + lat_part[o]

    total[here, :] = lax.fori_loop(1, n_lat, add_lat, lat_part[0])
    each(n_col, lambda o: total_copy(o, col).start())
    each(n_col, lambda o: total_copy(o, lax.rem(col + n_col - o, n_col)).wait_recv())
    stores = (
        pltpu.make_async_copy(total, total_out, store_sem.at[1]),
        pltpu.make_async_copy(observed_out, observed_store, store_sem.at[2]),
    )
    for copy in stores:
        copy.start()

    each(n_col, lambda o: part_copy(o).wait_send())
    each(n_lat, lambda o: lat_copy(o).wait_send())
    each(n_col, lambda o: total_copy(o, col).wait_send())
    for t in range(steps):
        each(half, lambda k: slot_copy(t, 0, k).wait_send())
        each(half, lambda k: slot_copy(t, 1, k).wait_send())
        table_copy(t).wait_send()
        for side in range(4):

            @pl.when(exists[side])
            def _():
                halo(t, side).wait_send()

    store.wait()
    for copy in stores:
        copy.wait()


def split(x):
    high = x.astype(jnp.bfloat16)
    return high, (x - high.astype(jnp.float32)).astype(jnp.bfloat16)


def transform_kernel(final, observed, total, final_out, observed_out, values, results, gram, square, load_sem, store_sem):
    cells, m = final.shape
    watched = observed.shape[0]
    f32 = jnp.float32
    load_gram = pltpu.make_async_copy(total, gram, load_sem.at[0])
    load_final = pltpu.make_async_copy(final, values.at[pl.ds(0, cells)], load_sem.at[1])
    load_observed = pltpu.make_async_copy(observed, values.at[pl.ds(cells, watched)], load_sem.at[2])
    load_gram.start()
    load_observed.start()
    load_final.start()

    row, lane = (lax.broadcasted_iota(jnp.int32, (m, m), axis) for axis in (0, 1))
    identity = jnp.where(row == lane, 1.0, 0.0).astype(f32)
    load_gram.wait()
    square[:, 0:m] = gram[0:m, :] + identity
    square[:, m:] = identity
    line = lax.broadcasted_iota(jnp.int32, (8, m), 0)
    for low in range(0, m, 8):
        left, right = square[low : low + 8, 0:m], square[low : low + 8, m:]
        pivots = [jnp.broadcast_to(left[:, low + k : low + k + 1], (8, m)) for k in range(8)]

        def spread(x, j):
            return jnp.broadcast_to(x[j : j + 1, :], (8, m))

        for j in range(8):
            pivot = spread(pivots[j], j)
            root = lax.rsqrt(pivot)
            root = root * (1.5 - 0.5 * pivot * root * root)
            column = jnp.where(line > j, pivots[j] * root, 0.0)
            here = line == j
            x, y = spread(left, j) * root, spread(right, j) * root
            left = jnp.where(here, x, left - column * x)
            right = jnp.where(here, y, right - column * y)
            for k in range(j + 1, 8):
                pivots[k] = pivots[k] - column * spread(column, k)
        square[low : low + 8, m:] = right
        if low + 8 < m:
            both = jnp.concatenate([left, right], axis=1)
            a = both.astype(jnp.bfloat16).astype(f32)
            b = (both - a).astype(jnp.bfloat16).astype(f32)
            c = (both - a) - b
            one = jnp.concatenate([t[:, 0:m] for t in (a, a, b, b, a, c)], axis=0)
            two = jnp.concatenate([a, b, a, b, c, a], axis=0)
            update = jnp.dot(
                jnp.transpose(one).astype(jnp.bfloat16), two.astype(jnp.bfloat16), preferred_element_type=f32
            )
            square[low + 8 :, :] = square[low + 8 :, :] - update[low + 8 :, :]
    inverse = square[:, m:]
    push = gram[m : m + 1, :]
    inner = jnp.sum(inverse * push, axis=1, keepdims=True)
    offset = jnp.sum(inverse * inner, axis=0, keepdims=True) / math.sqrt(m - 1.0)
    turned = inverse + offset
    turned = turned - jnp.mean(turned, axis=1, keepdims=True) + 1.0 / m
    high, low = split(jnp.transpose(turned))
    line = jnp.concatenate([high, low], axis=1)
    mix = jnp.concatenate([line, line], axis=0)

    def apply(at, size):
        high, low = split(values[pl.ds(at, size), :])
        both = jnp.dot(jnp.concatenate([high, low], axis=1), mix, preferred_element_type=f32)
        results[pl.ds(at, size), :] = both[:, 0:m] + both[:, m:]

    tile = cells // 16
    load_final.wait()
    load_observed.wait()

    def store(q):
        here = pl.ds(pl.multiple_of(q * tile, 8), tile)
        return pltpu.make_async_copy(results.at[here], final_out.at[here], store_sem.at[q])

    def one_tile(q, carry):
        apply(pl.multiple_of(q * tile, 8), tile)
        store(q).start()
        return carry

    apply(cells, watched)
    store_observed = pltpu.make_async_copy(results.at[pl.ds(cells, watched)], observed_out, store_sem.at[16])
    store_observed.start()
    lax.fori_loop(0, 16, one_tile, 0)
    store_observed.wait()

    def finish(q, carry):
        store(q).wait()
        return carry

    lax.fori_loop(0, 16, finish, 0)


def on_device(
    n_lat,
    n_col,
    control,
    perturbations,
    zonal_flow,
    meridional_flow,
    diffusivity,
    send_cell,
    send_station,
    send_weight,
    send_count,
    obs_value,
    obs_error,
):
    nx, ny, m = perturbations.shape
    cap = send_cell.shape[3]
    steps, owned = obs_value.shape
    rows = slice_rows(m, n_col)
    f32 = jnp.float32
    state = pltpu.VMEM((nx + 2, ny + 2 * PAD, m), f32)
    dma = pltpu.SemaphoreType.DMA
    anywhere = pl.BlockSpec(memory_space=pl.ANY)
    final, observed, total = pl.pallas_call(
        functools.partial(forecast_kernel, n_lat, n_col),
        out_shape=(
            jax.ShapeDtypeStruct((nx, ny, m), f32),
            jax.ShapeDtypeStruct((steps, owned, m), f32),
            jax.ShapeDtypeStruct((n_col * rows, m), f32),
        ),
        in_specs=[anywhere] * 11,
        out_specs=(anywhere,) * 3,
        scratch_shapes=[
            pltpu.VMEM((nx, ny), f32),
            pltpu.VMEM((nx, ny), f32),
            pltpu.VMEM((nx, ny), f32),
            pltpu.VMEM((nx, ny), f32),
            pltpu.SMEM((n_col, cap), jnp.int32),
            pltpu.VMEM((n_col, cap), jnp.int32),
            pltpu.VMEM((n_col, cap), f32),
            pltpu.SMEM((1, n_col), jnp.int32),
            pltpu.VMEM((steps, owned), f32),
            pltpu.VMEM((steps, owned), f32),
            pltpu.VMEM((steps, owned, m), f32),
            pltpu.VMEM((4, nx, ny, m), f32),
            state,
            state,
            state,
            pltpu.VMEM((ny, 128), f32),
            pltpu.VMEM((ny, 128), f32),
            pltpu.VMEM((steps, 2, nx, m), f32),
            pltpu.VMEM((steps, 2, nx, m), f32),
            pltpu.VMEM((steps, 2, ny, m), f32),
            pltpu.VMEM((steps, 2, n_col // 2, cap + 8, m), f32),
            pltpu.VMEM((steps, 2, n_col // 2, cap + 8, m), f32),
            pltpu.VMEM((steps, owned, m), f32),
            pltpu.VMEM((steps, owned, m), f32),
            pltpu.VMEM((n_col * rows, m), f32),
            pltpu.VMEM((n_col, rows, m), f32),
            pltpu.VMEM((n_lat, rows, m), f32),
            pltpu.VMEM((n_col * rows, m), f32),
            dma((10,)),
            dma((4,)),
            dma((3,)),
            dma((steps, 4)),
            dma((steps, 4)),
            dma((steps, 2, n_col // 2)),
            dma((steps, 2, n_col // 2)),
            dma((steps,)),
            dma((steps,)),
            dma((n_col,)),
            dma((n_col,)),
            dma((n_lat,)),
            dma((n_lat,)),
            dma((n_col,)),
            dma((n_col,)),
        ],
        compiler_params=pltpu.CompilerParams(
            collective_id=0, has_side_effects=True, vmem_limit_bytes=56 * 1024 * 1024
        ),
    )(
        control,
        perturbations,
        zonal_flow,
        meridional_flow,
        diffusivity,
        send_cell[0, 0],
        send_station[0, 0],
        send_weight[0, 0],
        send_count[0],
        obs_value,
        obs_error,
    )
    cells, watched = nx * ny, steps * owned
    analysis, obs_analysis = pl.pallas_call(
        transform_kernel,
        out_shape=(jax.ShapeDtypeStruct((cells, m), f32), jax.ShapeDtypeStruct((watched, m), f32)),
        in_specs=[anywhere] * 3,
        out_specs=(anywhere,) * 2,
        scratch_shapes=[
            pltpu.VMEM((cells + watched, m), f32),
            pltpu.VMEM((cells + watched, m), f32),
            pltpu.VMEM(total.shape, f32),
            pltpu.VMEM((m, 2 * m), f32),
            dma((3,)),
            dma((17,)),
        ],
        compiler_params=pltpu.CompilerParams(vmem_limit_bytes=60 * 1024 * 1024),
    )(final.reshape(cells, m), observed.reshape(watched, m), total)
    return analysis.reshape(nx, ny, m), obs_analysis.reshape(steps, owned, m)


def solution(mesh):
    n_lat, n_col = mesh.shape["lat"], mesh.shape["col"]
    return jax.shard_map(
        functools.partial(on_device, n_lat, n_col),
        mesh=mesh,
        in_specs=(
            P("lat", "col"),
            P("lat", "col", None),
            P("lat", "col"),
            P("lat", "col"),
            P("lat", "col"),
            P("lat", "col", None, None),
            P("lat", "col", None, None),
            P("lat", "col", None, None),
            P("lat", "col", None),
            P(None, ("lat", "col")),
            P(None, ("lat", "col")),
        ),
        out_specs=(P("lat", "col", None), P(None, ("lat", "col"), None)),
        check_vma=False,
    )
```
